256 devices in a mesh: fsdp: 16 (over x_lo, z), st: 16 (over y, x_hi, core).
Axes of the slice: x: 4 (x_hi: 2, x_lo: 2; x = x_hi * 2 + x_lo), y: 4, z: 8, core: 2. Of those that a mesh axis runs over, the one named last changes fastest.
Arguments:
- queries: bfloat16 [1, 24576, 2048], P(None, 'st', 'fsdp'), may hold values from -4.5 to 4.5
- key_rows: bfloat16 [1, 24576, 2048], P(None, 'st', 'fsdp'), may hold values from -4.5 to 4.5
- value_rows: bfloat16 [1, 24576, 2048], P(None, 'st', 'fsdp'), may hold values from -6 to 6
- out_grad: bfloat16 [1, 24576, 1536], P(None, 'st', 'fsdp'), may hold values from -6 to 6
- proj_weight: bfloat16 [2048, 1536], P('fsdp'), may hold values from -0.125 to 0.125
- pattern: int32 [64, 27], P('st'), may hold values from -1 to 63, as said below
Outputs:
- projected: bfloat16 [1, 24576, 1536], P(None, 'st', 'fsdp')
- query_grad: bfloat16 [1, 24576, 2048], P(None, 'st', 'fsdp')
- key_grad: bfloat16 [1, 24576, 2048], P(None, 'st', 'fsdp')
- value_grad: bfloat16 [1, 24576, 2048], P(None, 'st', 'fsdp')
- weight_grad: float32 [2048, 1536], P('fsdp', 'st')
The draws below stay inside these ranges and needn't reach their ends.
Inputs may be any that keep to these rules, and one draw needn't show every extreme that they name: Slot j stands for the offsets (j // 9 - 1) in frame, (j // 3 % 3 - 1) in tile row and (j % 3 - 1) in column; pattern[t, j] is -1 or the tile at t's frame, row and column plus those offsets, which lies inside the grid of 2 frames, 16 rows and 2 columns; slots 10, 13 and 16 are never -1 where that tile exists.
All inputs are finite; a program needn't handle non-finite values.
Results may differ from the reference program's by a relative error of at most 0.023.
Values may be sent and summed in bfloat16 or wider, within the bound.
No kernel may reach another device: no remote copies, remote signals or barrier semaphores. Data moves between devices by JAX's collectives and lax.ppermute only.
A program may use at most 128 MiB of HBM per device.

```python
from functools import partial
import jax
import jax.numpy as jnp
from jax import lax

HEADS = 16
HDIM = 128
DW = 1536
TILE = 384
TF = 2
TC = 2
NB = 27
VIDS = 1
HD = 2048
TILES = 64
TOKENS = 24576


def draw_queries(key, part):
    key = jax.random.fold_in(key, 11)
    values_out = jnp.clip(jax.random.normal(key, (VIDS, TILES, TILE, HD)), -4.5, 4.5)
    return values_out.reshape(VIDS, TOKENS, HD).astype(jnp.bfloat16)


def draw_key_rows(key, part):
    key = jax.random.fold_in(key, 12)
    values_out = jnp.clip(jax.random.normal(key, (VIDS, TILES, TILE, HD)), -4.5, 4.5)
    return values_out.reshape(VIDS, TOKENS, HD).astype(jnp.bfloat16)


def draw_pattern(key, part):
    key = jax.random.fold_in(key, 13)
    tile_ids = jnp.arange(TILES, dtype=jnp.int32)[:, None]
    slot_ids = jnp.arange(NB, dtype=jnp.int32)[None, :]
    tile_row = tile_ids // (TF * TC)
    tile_frame = tile_ids // TC % TF
    tile_col = tile_ids % TC
    near_row = tile_row + slot_ids // 3 % 3 - 1
    near_frame = tile_frame + slot_ids // 9 - 1
    near_col = tile_col + slot_ids % 3 - 1
    inside = (near_row >= 0) & (near_row < TILES // (TF * TC)) & (near_frame >= 0) & (near_frame < TF)
    inside = inside & (near_col >= 0) & (near_col < TC)
    always_on = (slot_ids // 9 == 1) & (slot_ids % 3 == 1)
    coin_flip = jax.random.randint(key, (TILES, NB), 0, 2)
    chosen = inside & (always_on | (coin_flip == 1))
    return jnp.where(chosen, (near_row * TF + near_frame) * TC + near_col, -1).astype(jnp.int32)


def with_spikes(drawn, key, source, target, shards_of, factor):
    def block_of(axis_at):
        return (jnp.arange(drawn.shape[axis_at]) // (drawn.shape[axis_at] // shards_of)).reshape((-1,) + (1,) * (drawn.ndim - 1 - axis_at))

    first = jax.random.permutation(key, shards_of)[block_of(target)]
    second = (block_of(target) + shards_of // 2) % shards_of
    return jnp.where((block_of(source) == first) | (block_of(source) == second), factor * drawn, drawn)


def shard_levels(key, dims, cuts, smallest, top_value):
    loudness, own = 1.0, jax.random.fold_in(key, 6)
    for dim, blocks in cuts:
        draws = jnp.exp(jax.random.uniform(jax.random.fold_in(own, dim), (blocks,), jnp.float32, smallest / len(cuts), top_value / len(cuts)))
        loudness = loudness * jnp.repeat(draws, dims[dim] // blocks).reshape([-1 if axis == dim else 1 for axis in range(len(dims))])
    return loudness


def gaussian(own_key, shape, width, reach, shards=(), kind=jnp.bfloat16):
    entries = jax.random.normal(own_key, shape, jnp.float32) * width
    if len(shards) > 0:
        entries = shard_levels(own_key, shape, shards, -0.22, 0.18) * entries
    return jnp.clip(entries, min=-reach, max=reach).astype(kind)


def noise_with(rng, dims, width, reach, pieces, heavy, kind=jnp.bfloat16):
    values = width * jax.random.normal(rng, dims, jnp.float32)
    if pieces:
        values = values * shard_levels(rng, dims, pieces, -0.22, 0.18)
    return jnp.clip(with_spikes(values, jax.random.fold_in(rng, 3), *heavy), -reach, reach).astype(kind)


def setup_inputs(seed: int = 0) -> dict:
    keys = jax.random.split(jax.random.key(seed), 7)
    return {
        "queries": draw_queries(jax.random.fold_in(keys[6], 71), 0),
        "key_rows": draw_key_rows(jax.random.fold_in(keys[6], 71), 0),
        "value_rows": gaussian(keys[2], (VIDS, TOKENS, HD), 1.0, 6.0, ((1, 16), (2, 16))),
        "out_grad": noise_with(keys[3], (VIDS, TOKENS, DW), 1.0, 6.0, ((1, 16), (2, 16)), (1, 2, 16, 2.0)),
        "proj_weight": gaussian(keys[4], (HD, DW), HD ** -0.5, 0.125, ((0, 16),)),
        "pattern": draw_pattern(jax.random.fold_in(keys[6], 71), 0),
    }


def widened(array):
    return lax.optimization_barrier(array).astype(jnp.float32)


def one_video(proj_weight, pattern, video_items):
    queries, key_rows, value_rows, out_grad = video_items
    scaling = HDIM ** -0.5
    row_tiles = TF * TC
    row_tokens = row_tiles * TILE
    tile_rows = TILES // row_tiles
    offsets = jnp.arange(3 * row_tiles, dtype=jnp.int32)
    back_rows = jnp.dot(out_grad, proj_weight.T, preferred_element_type=jnp.float32).astype(jnp.bfloat16)
    padded_keys = jnp.pad(key_rows, ((row_tokens, row_tokens), (0, 0)))
    padded_values = jnp.pad(value_rows, ((row_tokens, row_tokens), (0, 0)))

    def one_row(carry, row):
        start = (row * row_tokens).astype(jnp.int32)
        query_block = lax.dynamic_slice_in_dim(queries, start, row_tokens, 0)
        query_block = query_block.reshape(row_tokens, HEADS, HDIM).astype(jnp.float32)
        back_block = widened(lax.dynamic_slice_in_dim(back_rows, start, row_tokens, 0)).reshape(row_tokens, HEADS, HDIM)
        key_band = lax.dynamic_slice_in_dim(padded_keys, start, 3 * row_tokens, 0)
        key_band = key_band.reshape(3 * row_tokens, HEADS, HDIM).astype(jnp.float32)
        value_band = lax.dynamic_slice_in_dim(padded_values, start, 3 * row_tokens, 0)
        value_band = value_band.reshape(3 * row_tokens, HEADS, HDIM).astype(jnp.float32)
        tile_ids = (row - 1) * row_tiles + offsets
        band_row = row - 1 + offsets // row_tiles
        valid = (band_row >= 0) & (band_row < tile_rows)
        rows_pattern = lax.dynamic_slice_in_dim(pattern, (row * row_tiles).astype(jnp.int32), row_tiles, 0)
        listed = valid[None, :] & jnp.any(rows_pattern[:, None, :] == tile_ids[None, :, None], axis=2)
        token_mask = jnp.repeat(jnp.repeat(listed, TILE, axis=0), TILE, axis=1)
        scores = jnp.einsum("ihd,khd->hik", query_block, key_band) * scaling
        scores = jnp.where(token_mask[None], scores, -jnp.inf)
        peak_score = jnp.max(scores, axis=2, keepdims=True)
        raised = jnp.exp(scores - peak_score)
        probability = raised / jnp.sum(raised, axis=2, keepdims=True)
        weights = widened(probability.astype(jnp.bfloat16))
        attended = jnp.einsum("hik,khd->ihd", weights, value_band).astype(jnp.bfloat16)
        prob_grad = jnp.einsum("ihd,khd->hik", back_block, value_band)
        row_delta = jnp.einsum("ihd,ihd->hi", back_block, widened(attended))
        score_grad = widened((probability * (prob_grad - row_delta[:, :, None])).astype(jnp.bfloat16))
        query_grad = (scaling * jnp.einsum("hik,khd->ihd", score_grad, key_band)).astype(jnp.bfloat16)
        value_part = jnp.einsum("hik,ihd->khd", weights, back_block)
        key_part = jnp.einsum("hik,ihd->khd", score_grad, query_block)
        band_grads = jnp.stack((key_part, value_part)).reshape(2, 3 * row_tokens, HD)
        current = lax.dynamic_slice_in_dim(carry, start, 3 * row_tokens, 1)
        carry = lax.dynamic_update_slice_in_dim(carry, current + band_grads, start, 1)
        return carry, (attended.reshape(row_tokens, HD), query_grad.reshape(row_tokens, HD))

    initial = jnp.zeros((2, TOKENS + 2 * row_tokens, HD), jnp.float32)
    carry, (attended, query_grad) = lax.scan(one_row, initial, jnp.arange(tile_rows, dtype=jnp.int32))
    flat_out = attended.reshape(TOKENS, HD)
    projected = jnp.dot(flat_out, proj_weight, preferred_element_type=jnp.float32).astype(jnp.bfloat16)
    key_grad = (scaling * carry[0, row_tokens:row_tokens + TOKENS]).astype(jnp.bfloat16)
    value_grad = carry[1, row_tokens:row_tokens + TOKENS].astype(jnp.bfloat16)
    return projected, query_grad.reshape(TOKENS, HD), key_grad, value_grad, flat_out


def reference(queries, key_rows, value_rows, out_grad, proj_weight, pattern):
    results = lax.map(partial(one_video, proj_weight, pattern), (queries, key_rows, value_rows, out_grad))
    projected, query_grad, key_grad, value_grad, attended = results
    weight_grad = jnp.dot(attended.reshape(VIDS * TOKENS, HD).T, out_grad.reshape(VIDS * TOKENS, DW),
                          preferred_element_type=jnp.float32)
    return projected, query_grad, key_grad, value_grad, weight_grad
```

```python
import functools

import jax
import jax.numpy as jnp
from jax import lax
from jax.experimental import pallas as pl
from jax.experimental.pallas import tpu as pltpu
from jax.sharding import Mesh
from jax.sharding import PartitionSpec as P

HDIM = 128
TILE = 384
TF = 2
TC = 2
ROW_TILES = TF * TC
BAND = 3 * ROW_TILES
SCALING = HDIM ** (-0.5)
LOG2E = 1.4426950408889634
BF = jnp.bfloat16
F32 = jnp.float32
ST = ("y", "xh", "core")
NT = (((1,), (1,)), ((), ()))
TN = (((0,), (0,)), ((), ()))
NN = (((1,), (0,)), ((), ()))


def dot(a, b, dims):
    return lax.dot_general(a, b, dims, preferred_element_type=F32)


def build_list(pattern_ref, list_ref, tile):
    frame, col = tile // TC, tile % TC
    count = jnp.int32(0)
    for place in range(BAND):
        row, key_frame, key_col = place // ROW_TILES, place // TC % TF, place % TC
        slot = (key_frame - frame + 1) * 9 + row * 3 + (key_col - col + 1)
        list_ref[tile, count] = jnp.int32(place)
        count = count + (pattern_ref[tile, slot] >= 0).astype(jnp.int32)
    return count


def fill_band(refs, band, sem):
    copies = [
        pltpu.make_async_copy(ref, band.at[pl.ds(i * ROW_TILES, ROW_TILES)], sem.at[i])
        for i, ref in enumerate(refs)
    ]
    for copy in copies:
        copy.start()
    return copies


def forward_kernel(
    pattern_ref, q_ref, ka_ref, ko_ref, kb_ref, va_ref, vo_ref, vb_ref,
    att_ref, lse_ref,
    kband, vband, list_ref, top, total, acc, ksem, vsem,
):
    copies = fill_band((ka_ref, ko_ref, kb_ref), kband, ksem)
    copies += fill_band((va_ref, vo_ref, vb_ref), vband, vsem)
    counts = [build_list(pattern_ref, list_ref, t) for t in range(ROW_TILES)]
    for copy in copies:
        copy.wait()
    for tile in range(ROW_TILES):
        top[...] = jnp.full(top.shape, -jnp.inf, F32)
        total[...] = jnp.zeros(total.shape, F32)
        acc[...] = jnp.zeros(acc.shape, F32)

        def step(i, carry):
            place = list_ref[tile, i]
            scores = dot(q_ref[tile], kband[place], NT) * (SCALING * LOG2E)
            before = top[...]
            peak = jnp.maximum(before, jnp.max(scores, axis=1, keepdims=True))
            raised = jnp.exp2(scores - peak)
            shrink = jnp.exp2(before - peak)
            top[...] = peak
            total[...] = shrink * total[...] + jnp.sum(raised, axis=1, keepdims=True)
            acc[...] = shrink * acc[...] + dot(raised.astype(BF), vband[place], NN)
            return carry

        lax.fori_loop(0, counts[tile], step, 0)
        att_ref[tile] = (acc[...] / total[...]).astype(BF)
        lse = top[...] + jnp.log2(total[...])
        lse_ref[tile] = jnp.broadcast_to(lse, (TILE, HDIM)).T[:8]


def backward_kernel(
    pattern_ref, q_ref, ka_ref, ko_ref, kb_ref, va_ref, vo_ref, vb_ref,
    back_ref, att_ref, lse_ref,
    dq_ref, up_ref, down_ref, own_ref,
    kband, vband, list_ref, dk, dv, dq, ksem, vsem,
):
    copies = fill_band((ka_ref, ko_ref, kb_ref), kband, ksem)
    copies += fill_band((va_ref, vo_ref, vb_ref), vband, vsem)
    counts = [build_list(pattern_ref, list_ref, t) for t in range(ROW_TILES)]
    dk[...] = jnp.zeros(dk.shape, F32)
    dv[...] = jnp.zeros(dv.shape, F32)
    for copy in copies:
        copy.wait()
    for tile in range(ROW_TILES):
        dq[...] = jnp.zeros(dq.shape, F32)
        prod = back_ref[tile].astype(F32) * att_ref[tile].astype(F32)
        delta = jnp.sum(prod.T, axis=0, keepdims=True)
        lse = lse_ref[tile][:1]

        def step(i, carry):
            place = list_ref[tile, i]
            queries, back = q_ref[tile], back_ref[tile]
            keys, values = kband[place], vband[place]
            scores = dot(keys, queries, NT) * (SCALING * LOG2E)
            prob = jnp.exp2(scores - lse)
            dv[place] += dot(prob.astype(BF), back, NN)
            prob_grad = dot(values, back, NT)
            score_grad = (prob * (prob_grad - delta)).astype(BF)
            dk[place] += dot(score_grad, queries, NN)
            dq[...] += dot(score_grad, keys, TN)
            return carry

        lax.fori_loop(0, counts[tile], step, 0)
        dq_ref[tile] = (dq[...] * SCALING).astype(BF)
    for i in range(ROW_TILES):
        up_ref[0, i] = dk[i].astype(BF)
        up_ref[1, i] = dv[i].astype(BF)
        down_ref[0, i] = dk[2 * ROW_TILES + i].astype(BF)
        down_ref[1, i] = dv[2 * ROW_TILES + i].astype(BF)
        own_ref[0, i] = dk[ROW_TILES + i]
        own_ref[1, i] = dv[ROW_TILES + i]


VMEM_SPEC = pl.BlockSpec(memory_space=pltpu.VMEM)
SMEM_SPEC = pl.BlockSpec(memory_space=pltpu.SMEM)
ANY_SPEC = pl.BlockSpec(memory_space=pl.ANY)
BLOCK = (ROW_TILES, TILE, HDIM)
BAND_SCRATCH = [
    pltpu.VMEM((BAND, TILE, HDIM), BF),
    pltpu.VMEM((BAND, TILE, HDIM), BF),
    pltpu.SMEM((ROW_TILES, BAND + 1), jnp.int32),
]
PARAMS = pltpu.CompilerParams(vmem_limit_bytes=40 * 1024 * 1024)


def forward(pattern, queries, band):
    return pl.pallas_call(
        forward_kernel,
        name="attention_forward",
        out_shape=(
            jax.ShapeDtypeStruct(BLOCK, BF),
            jax.ShapeDtypeStruct((ROW_TILES, 8, TILE), F32),
        ),
        in_specs=[SMEM_SPEC, VMEM_SPEC] + [ANY_SPEC] * 6,
        out_specs=(VMEM_SPEC, VMEM_SPEC),
        scratch_shapes=BAND_SCRATCH
        + [
            pltpu.VMEM((TILE, 1), F32),
            pltpu.VMEM((TILE, 1), F32),
            pltpu.VMEM((TILE, HDIM), F32),
            pltpu.SemaphoreType.DMA((3,)),
            pltpu.SemaphoreType.DMA((3,)),
        ],
        compiler_params=PARAMS,
        cost_estimate=pl.CostEstimate(
            flops=3_000_000_000, bytes_accessed=4_000_000, transcendentals=7_000_000
        ),
    )(pattern, queries, *band)


def backward(pattern, queries, band, back, attended, lse):
    return pl.pallas_call(
        backward_kernel,
        name="attention_backward",
        out_shape=(
            jax.ShapeDtypeStruct(BLOCK, BF),
            jax.ShapeDtypeStruct((2,) + BLOCK, BF),
            jax.ShapeDtypeStruct((2,) + BLOCK, BF),
            jax.ShapeDtypeStruct((2,) + BLOCK, F32),
        ),
        in_specs=[SMEM_SPEC, VMEM_SPEC] + [ANY_SPEC] * 6 + [VMEM_SPEC] * 3,
        out_specs=(VMEM_SPEC,) * 4,
        scratch_shapes=BAND_SCRATCH
        + [
            pltpu.VMEM((BAND, TILE, HDIM), F32),
            pltpu.VMEM((BAND, TILE, HDIM), F32),
            pltpu.VMEM((TILE, HDIM), F32),
            pltpu.SemaphoreType.DMA((3,)),
            pltpu.SemaphoreType.DMA((3,)),
        ],
        compiler_params=PARAMS,
        cost_estimate=pl.CostEstimate(
            flops=8_000_000_000, bytes_accessed=8_000_000, transcendentals=7_000_000
        ),
    )(pattern, queries, *band, back, attended, lse)


def shifted(block, distance):
    route = [(i - distance, i) for i in range(16) if 0 <= i - distance < 16]
    return lax.ppermute(block, ST, route)


def swapped(block):
    return lax.ppermute(block, "xl", [(0, 1), (1, 0)])


def body(queries, key_rows, value_rows, out_grad, proj_weight, pattern):
    half = lax.axis_index("xl")
    tokens = queries.shape[1]
    q = queries.reshape(BLOCK)
    kv = jnp.stack((key_rows.reshape(BLOCK), value_rows.reshape(BLOCK)))
    above, below = shifted(kv, 1), shifted(kv, -1)
    band = (above[0], kv[0], below[0], above[1], kv[1], below[1])

    grad_half = lax.all_gather(out_grad[0].T, "z", axis=0, tiled=True)
    feats = grad_half.shape[0]
    w_mine = lax.dynamic_slice_in_dim(proj_weight, half * feats, feats, 1)
    w_other = swapped(lax.dynamic_slice_in_dim(proj_weight, (1 - half) * feats, feats, 1))

    attended, lse = forward(pattern, q, band)
    att = attended.reshape(tokens, HDIM)
    att_other = swapped(att)

    back_other = lax.dot_general(grad_half, w_other, (((0,), (1,)), ((), ())),
                                 preferred_element_type=F32).astype(BF)
    back_got = swapped(back_other)
    back_mine = lax.dot_general(grad_half, w_mine, (((0,), (1,)), ((), ())),
                                preferred_element_type=F32)
    back = (back_mine + back_got.astype(F32)).astype(BF)

    part = lax.dot_general(w_mine, att, (((0,), (1,)), ((), ())), preferred_element_type=F32)
    part = part + lax.dot_general(
        w_other, att_other, (((0,), (1,)), ((), ())), preferred_element_type=F32
    )
    projected = lax.psum_scatter(part.astype(BF), "z", scatter_dimension=0, tiled=True)
    projected = projected.T[None]

    wg_mine = dot(grad_half, att, NN).astype(BF)
    wg_other = dot(grad_half, att_other, NN).astype(BF)
    first = jnp.where(half == 0, wg_mine, wg_other)
    second = jnp.where(half == 0, wg_other, wg_mine)
    pieces = jnp.stack((first, second)).reshape(16, 96, HDIM)
    pieces = lax.all_to_all(pieces, ST, 0, 0, tiled=True)
    summed = jnp.sum(pieces.astype(F32), axis=0)
    route = [
        (h * 4 + 2 * a + y, a * 4 + 2 * h + y)
        for h in range(2)
        for a in range(2)
        for y in range(2)
    ]
    weight_grad = lax.ppermute(summed, ("xl", "y"), route).T

    dq, up, down, own = backward(
        pattern, q, band, back.reshape(BLOCK), attended, lse
    )
    total = own + shifted(up, -1).astype(F32) + shifted(down, 1).astype(F32)
    shape = (1, tokens, HDIM)
    key_grad = (SCALING * total[0]).astype(BF).reshape(shape)
    value_grad = total[1].astype(BF).reshape(shape)
    return projected, dq.reshape(shape), key_grad, value_grad, weight_grad


def solution(mesh):
    fine = Mesh(mesh.devices.reshape(2, 8, 4, 2, 2), ("xl", "z", "y", "xh", "core"))
    fsdp = ("xl", "z")
    rows = P(None, ST, fsdp)
    return jax.shard_map(
        body,
        mesh=fine,
        in_specs=(rows, rows, rows, rows, P(fsdp, None), P(ST, None)),
        out_specs=(rows, rows, rows, rows, P(fsdp, ST)),
        check_vma=False,
    )
```

```python
import functools

import jax
import jax.numpy as jnp
from jax import lax
from jax.experimental import pallas as pl
from jax.experimental.pallas import tpu as pltpu
from jax.sharding import Mesh
from jax.sharding import PartitionSpec as P

HDIM = 128
TILE = 384
TF = 2
TC = 2
ROW_TILES = TF * TC
BAND = 3 * ROW_TILES
SCALING = HDIM ** (-0.5)
LOG2E = 1.4426950408889634
BF = jnp.bfloat16
F32 = jnp.float32
ST = ("y", "xh", "core")
NT = (((1,), (1,)), ((), ()))
TN = (((0,), (0,)), ((), ()))
NN = (((1,), (0,)), ((), ()))


def dot(a, b, dims):
    return lax.dot_general(a, b, dims, preferred_element_type=F32)


def build_pairs(pattern_ref, tile_of, place_of, rows):
    count = jnp.int32(0)
    for tile in range(ROW_TILES):
        frame, col = tile // TC, tile % TC
        for at, row in enumerate(rows):
            for inner in range(ROW_TILES):
                slot = (inner // TC - frame + 1) * 9 + row * 3 + (inner % TC - col + 1)
                tile_of[count] = jnp.int32(tile)
                place_of[count] = jnp.int32(at * ROW_TILES + inner)
                count = count + (pattern_ref[tile, slot] >= 0).astype(jnp.int32)
    return count


def run_pairs(count, make, use, even, odd):
    make(even, 0)

    def step(j, carry):
        i = 2 * j
        make(odd, i + 1)
        use(even, i)
        make(even, i + 2)
        use(odd, i + 1)
        return carry

    lax.fori_loop(0, (count - 1) // 2, step, 0)

    @pl.when(count % 2 == 1)
    def _():
        use(even, count - 1)

    @pl.when(count % 2 == 0)
    def _():
        make(odd, count - 1)
        use(even, count - 2)
        use(odd, count - 1)


def fill_band(refs, kband, vband, sem):
    copies = []
    for i, ref in enumerate(refs):
        place = pl.ds(i * ROW_TILES, ROW_TILES)
        copies.append(pltpu.make_async_copy(ref.at[0], kband.at[place], sem.at[2 * i]))
        copies.append(pltpu.make_async_copy(ref.at[1], vband.at[place], sem.at[2 * i + 1]))
    for copy in copies:
        copy.start()
    return copies


def forward_pairs(count, q_ref, kband, vband, tile_of, place_of, even, odd, top, total, acc):
    def make(slot, i):
        scores = dot(kband[place_of[i]], q_ref[tile_of[i]], NT) * (SCALING * LOG2E)
        slot[0][...] = scores
        slot[1][...] = jnp.max(scores, axis=0, keepdims=True)

    def use(slot, i):
        tile = tile_of[i]
        before = top[tile]
        peak = jnp.maximum(before, slot[1][...])
        shrink = jnp.exp2(before - peak)
        raised = jnp.exp2(slot[0][...] - peak)
        top[tile] = peak
        total[tile] = shrink * total[tile] + jnp.sum(raised, axis=0, keepdims=True)
        acc[tile] = shrink * acc[tile] + dot(vband[place_of[i]], raised.astype(BF), TN)

    run_pairs(count, make, use, even, odd)


def forward_own_kernel(
    pattern_ref, q_ref, k_ref, v_ref, top, total, acc, tile_of, place_of, s0, s1, m0, m1
):
    count = build_pairs(pattern_ref, tile_of, place_of, (1,))
    top[...] = jnp.full(top.shape, -jnp.inf, F32)
    total[...] = jnp.zeros(total.shape, F32)
    acc[...] = jnp.zeros(acc.shape, F32)
    forward_pairs(
        count, q_ref, k_ref, v_ref, tile_of, place_of, (s0, m0), (s1, m1), top, total, acc
    )


def forward_halo_kernel(
    pattern_ref, q_ref, top_in, total_in, acc_in, above_ref, below_ref, early_ref,
    att_ref, flip_ref, lse_ref,
    kband, vband, tile_of, place_of, s0, s1, m0, m1, top, total, acc, sem,
):
    copies = fill_band((above_ref, below_ref), kband, vband, sem)
    count = build_pairs(pattern_ref, tile_of, place_of, (0, 2))
    top[...] = top_in[...]
    total[...] = total_in[...]
    acc[...] = acc_in[...]
    for copy in copies:
        copy.wait()
    forward_pairs(
        count, q_ref, kband, vband, tile_of, place_of, (s0, m0), (s1, m1), top, total, acc
    )
    for tile in range(ROW_TILES):
        attended = acc[tile] / total[tile]
        flip_ref[tile] = attended.astype(BF)
        att_ref[tile] = attended.T.astype(BF)
        lse_ref[tile] = top[tile] + jnp.log2(total[tile])


def backward_pairs(
    count, q_ref, back, att_ref, lse_ref, kband, vband, tile_of, place_of,
    even, odd, delta, dk, dv, dq,
):
    for tile in range(ROW_TILES):
        prod = back[tile].astype(F32) * att_ref[tile].astype(F32)
        delta[tile] = jnp.sum(prod, axis=0, keepdims=True)

    def make(slot, i):
        tile, place = tile_of[i], place_of[i]
        scores = dot(kband[place], q_ref[tile], NT) * (SCALING * LOG2E)
        prob = jnp.exp2(scores - lse_ref[tile])
        prob_grad = dot(vband[place], back[tile], NN)
        slot[0][...] = prob.astype(BF)
        slot[1][...] = (prob * (prob_grad - delta[tile])).astype(BF)

    def use(slot, i):
        tile, place = tile_of[i], place_of[i]
        dv[place] += dot(slot[0][...], back[tile], NT)
        dk[place] += dot(slot[1][...], q_ref[tile], NN)
        dq[tile] += dot(kband[place], slot[1][...], TN)

    run_pairs(count, make, use, even, odd)


def backward_halo_kernel(
    pattern_ref, q_ref, back_mine_ref, back_got_ref, att_ref, lse_ref, above_ref, below_ref,
    early_ref,
    up_ref, down_ref, dq, back_ref, zero_ref,
    kband, vband, tile_of, place_of, p0, p1, d0, d1, delta, dk, dv, sem,
):
    copies = fill_band((above_ref, below_ref), kband, vband, sem)
    count = build_pairs(pattern_ref, tile_of, place_of, (0, 2))
    dk[...] = jnp.zeros(dk.shape, F32)
    dv[...] = jnp.zeros(dv.shape, F32)
    dq[...] = jnp.zeros(dq.shape, F32)
    zero_ref[...] = jnp.zeros(zero_ref.shape, F32)
    for tile in range(ROW_TILES):
        cols = pl.ds(tile * TILE, TILE)
        back_ref[tile] = (back_mine_ref[:, cols] + back_got_ref[:, cols].astype(F32)).astype(BF)
    for copy in copies:
        copy.wait()
    backward_pairs(
        count, q_ref, back_ref, att_ref, lse_ref, kband, vband, tile_of, place_of,
        (p0, d0), (p1, d1), delta, dk, dv, dq,
    )
    for i in range(ROW_TILES):
        up_ref[0, i] = dk[i].astype(BF)
        up_ref[1, i] = dv[i].astype(BF)
        down_ref[0, i] = dk[ROW_TILES + i].astype(BF)
        down_ref[1, i] = dv[ROW_TILES + i].astype(BF)


def backward_own_kernel(
    pattern_ref, q_ref, back_ref, att_ref, lse_ref, k_ref, v_ref, dq_in, early_ref,
    dq_ref, dk, dv, zero_ref,
    tile_of, place_of, p0, p1, d0, d1, delta, dq,
):
    count = build_pairs(pattern_ref, tile_of, place_of, (1,))
    dk[...] = jnp.zeros(dk.shape, F32)
    dv[...] = jnp.zeros(dv.shape, F32)
    zero_ref[...] = jnp.zeros(zero_ref.shape, F32)
    dq[...] = dq_in[...]
    backward_pairs(
        count, q_ref, back_ref, att_ref, lse_ref, k_ref, v_ref, tile_of, place_of,
        (p0, d0), (p1, d1), delta, dk, dv, dq,
    )
    for tile in range(ROW_TILES):
        dq_ref[tile] = (dq[tile] * SCALING).T.astype(BF)


def weight_kernel(place_ref, grad_ref, att_ref, other_ref, early_ref, send_ref, keep_ref, heads, total):
    half, core = place_ref[0], place_ref[1]
    heads[:, pl.ds(pl.multiple_of(half * HDIM, HDIM), HDIM)] = att_ref[...]
    heads[:, pl.ds(pl.multiple_of((1 - half) * HDIM, HDIM), HDIM)] = other_ref[...]
    total[...] = dot(grad_ref[...], heads[...], NN)
    rows = send_ref.shape[3]
    for low in range(2):
        for xh in range(2):
            chunk = low * 4 + xh * 2
            mine = pl.ds(pl.multiple_of((chunk + core) * rows, 8), rows)
            yours = pl.ds(pl.multiple_of((chunk + 1 - core) * rows, 8), rows)
            for a in range(2):
                lanes = slice(a * HDIM, (a + 1) * HDIM)
                keep_ref[a, low, xh] = total[mine, lanes]
                send_ref[a, low, xh] = total[yours, lanes].astype(BF)


VM = pl.BlockSpec(memory_space=pltpu.VMEM)
SM = pl.BlockSpec(memory_space=pltpu.SMEM)
HB = pl.BlockSpec(memory_space=pltpu.HBM)
BLOCK = (ROW_TILES, TILE, HDIM)
FLIP = (ROW_TILES, HDIM, TILE)
LINE = (ROW_TILES, 1, TILE)
HALO = (2 * ROW_TILES, TILE, HDIM)
PAIR_LISTS = [pltpu.SMEM((49,), jnp.int32), pltpu.SMEM((49,), jnp.int32)]
HALO_BAND = [pltpu.VMEM(HALO, BF), pltpu.VMEM(HALO, BF)]
SCORES = [pltpu.VMEM((TILE, TILE), F32)] * 2 + [pltpu.VMEM((1, TILE), F32)] * 2
TERMS = [pltpu.VMEM((TILE, TILE), BF)] * 4
DMA_SEMS = pltpu.SemaphoreType.DMA((4,))


def kernel_call(kernel, name, outs, in_specs, scratch, flops):
    return pl.pallas_call(
        kernel,
        name=name,
        out_shape=tuple(jax.ShapeDtypeStruct(shape, kind) for shape, kind in outs),
        in_specs=in_specs,
        out_specs=(VM,) * len(outs),
        scratch_shapes=scratch,
        compiler_params=pltpu.CompilerParams(vmem_limit_bytes=32 * 1024 * 1024),
        cost_estimate=pl.CostEstimate(
            flops=flops, bytes_accessed=4_000_000, transcendentals=3_000_000
        ),
    )


def forward_own(*args):
    return kernel_call(
        forward_own_kernel, "forward_own", [(LINE, F32), (LINE, F32), (FLIP, F32)],
        [SM, VM, VM, VM], PAIR_LISTS + SCORES, 3_000_000_000,
    )(*args)


def forward_halo(*args):
    state = [pltpu.VMEM(LINE, F32), pltpu.VMEM(LINE, F32), pltpu.VMEM(FLIP, F32)]
    return kernel_call(
        forward_halo_kernel, "forward_halo", [(BLOCK, BF), (FLIP, BF), (LINE, F32)],
        [SM] + [VM] * 4 + [HB] * 3, HALO_BAND + PAIR_LISTS + SCORES + state + [DMA_SEMS],
        5_000_000_000,
    )(*args)


def backward_halo(*args):
    outs = [((2,) + BLOCK, BF), ((2,) + BLOCK, BF), (FLIP, F32), (FLIP, BF), ((1, HDIM), F32)]
    return kernel_call(
        backward_halo_kernel, "backward_halo", outs, [SM] + [VM] * 5 + [HB] * 3,
        HALO_BAND + PAIR_LISTS + TERMS
        + [pltpu.VMEM(LINE, F32), pltpu.VMEM(HALO, F32), pltpu.VMEM(HALO, F32), DMA_SEMS],
        12_000_000_000,
    )(*args)


def backward_own(*args):
    outs = [(BLOCK, BF), (BLOCK, F32), (BLOCK, F32), ((1, HDIM), F32)]
    return kernel_call(
        backward_own_kernel, "backward_own", outs, [SM] + [VM] * 7 + [HB],
        PAIR_LISTS + TERMS + [pltpu.VMEM(LINE, F32), pltpu.VMEM(FLIP, F32)],
        6_000_000_000,
    )(*args)


def weight_parts(place, grad_half, att, att_other, early):
    feats, tokens = grad_half.shape
    shape = (2, 2, 2, feats // 8, HDIM)
    return kernel_call(
        weight_kernel, "weight_parts", [(shape, BF), (shape, F32)], [SM] + [VM] * 3 + [HB],
        [pltpu.VMEM((tokens, 2 * HDIM), BF), pltpu.VMEM((feats, 2 * HDIM), F32)],
        2_000_000_000,
    )(place, grad_half, att, att_other, early)


def shifted(block, distance):
    route = [(i - distance, i) for i in range(16) if 0 <= i - distance < 16]
    return lax.ppermute(block, ST, route)


def swapped(block):
    return lax.ppermute(block, "xl", [(0, 1), (1, 0)])


def halved(part, axis, distance, size, dim, bit):
    route = [(i, i ^ distance) for i in range(size)]
    send = lax.dynamic_index_in_dim(part, 1 - bit, dim, keepdims=False).astype(BF)
    keep = lax.dynamic_index_in_dim(part, bit, dim, keepdims=False)
    return keep, lax.ppermute(send, axis, route)


def body(queries, key_rows, value_rows, out_grad, proj_weight, pattern):
    half, y = lax.axis_index("xl"), lax.axis_index("y")
    tokens = queries.shape[1]
    q = queries.reshape(BLOCK)
    keys, values = key_rows.reshape(BLOCK), value_rows.reshape(BLOCK)
    kv = jnp.stack((keys, values))
    above, below = shifted(kv, 1), shifted(kv, -1)

    grad_half = lax.all_gather(out_grad[0].T, "z", axis=0, tiled=True)
    feats = grad_half.shape[0]
    w_mine = lax.dynamic_slice_in_dim(proj_weight, half * feats, feats, 1)
    w_other = swapped(lax.dynamic_slice_in_dim(proj_weight, (1 - half) * feats, feats, 1))

    own_state = forward_own(pattern, q, keys, values)
    attended, att_flip, lse = forward_halo(pattern, q, *own_state, above, below, w_other)
    att = attended.reshape(tokens, HDIM)
    att_other = swapped(att)

    back_sent = dot(w_other, grad_half, NN).astype(BF)
    back_got = swapped(back_sent)
    back_mine = dot(w_mine, grad_half, NN)

    by_rows = (((0,), (1,)), ((), ()))
    part = dot(w_mine, att, by_rows) + dot(w_other, att_other, by_rows)
    projected = lax.psum_scatter(part.astype(BF), "z", scatter_dimension=0, tiled=True)
    projected = projected.T[None]

    place = jnp.stack((half, lax.axis_index("core"))).astype(jnp.int32)
    sent, kept = weight_parts(place, grad_half, att, att_other, back_sent)
    got = lax.ppermute(sent, "core", [(0, 1), (1, 0)])
    kept, got = halved(kept + got.astype(F32), "xh", 1, 2, 2, lax.axis_index("xh"))

    up, down, dq_part, back, zero = backward_halo(
        pattern, q, back_mine, back_got, att_flip, lse, above, below, sent
    )
    kept, got = halved(kept + got.astype(F32) + zero, "y", 1, 4, 1, y % 2)
    up, down = shifted(up, -1), shifted(down, 1)

    dq, dk, dv, zero = backward_own(
        pattern, q, back, att_flip, lse, keys, values, dq_part, kept
    )
    kept, got = halved(kept + got.astype(F32) + zero, "y", 2, 4, 0, y // 2)
    summed = kept + got.astype(F32)
    route = [
        (h * 4 + 2 * a + low, a * 4 + 2 * h + low)
        for h in range(2)
        for a in range(2)
        for low in range(2)
    ]
    weight_grad = lax.ppermute(summed, ("xl", "y"), route).T

    shape = (1, tokens, HDIM)
    key_grad = SCALING * (dk + up[0].astype(F32) + down[0].astype(F32))
    value_grad = dv + up[1].astype(F32) + down[1].astype(F32)
    key_grad = key_grad.astype(BF).reshape(shape)
    value_grad = value_grad.astype(BF).reshape(shape)
    return projected, dq.reshape(shape), key_grad, value_grad, weight_grad


def solution(mesh):
    fine = Mesh(mesh.devices.reshape(2, 8, 4, 2, 2), ("xl", "z", "y", "xh", "core"))
    fsdp = ("xl", "z")
    rows = P(None, ST, fsdp)
    return jax.shard_map(
        body,
        mesh=fine,
        in_specs=(rows, rows, rows, rows, P(fsdp, None), P(ST, None)),
        out_specs=(rows, rows, rows, rows, P(fsdp, ST)),
        check_vma=False,
    )
```

```python
import functools

import jax
import jax.numpy as jnp
from jax import lax
from jax.experimental import pallas as pl
from jax.experimental.pallas import tpu as pltpu
from jax.sharding import Mesh
from jax.sharding import PartitionSpec as P

HDIM = 128
TILE = 384
TF = 2
TC = 2
ROW_TILES = TF * TC
BAND = 3 * ROW_TILES
SCALING = HDIM ** (-0.5)
LOG2E = 1.4426950408889634
BF = jnp.bfloat16
F32 = jnp.float32
ST = ("y", "xh", "core")
NT = (((1,), (1,)), ((), ()))
TN = (((0,), (0,)), ((), ()))
NN = (((1,), (0,)), ((), ()))


def dot(a, b, dims):
    return lax.dot_general(a, b, dims, preferred_element_type=F32)


def build_pairs(pattern_ref, tile_of, place_of, rows):
    count = jnp.int32(0)
    for tile in range(ROW_TILES):
        frame, col = tile // TC, tile % TC
        for at, row in enumerate(rows):
            for inner in range(ROW_TILES):
                slot = (inner // TC - frame + 1) * 9 + row * 3 + (inner % TC - col + 1)
                tile_of[count] = jnp.int32(tile)
                place_of[count] = jnp.int32(at * ROW_TILES + inner)
                count = count + (pattern_ref[tile, slot] >= 0).astype(jnp.int32)
    return count


def run_pairs(count, make, use, even, odd):
    @pl.when(count > 0)
    def _():
        make(even, 0)

    def step(j, carry):
        i = 2 * j
        make(odd, i + 1)
        use(even, i)
        make(even, i + 2)
        use(odd, i + 1)
        return carry

    lax.fori_loop(0, (count - 1) // 2, step, 0)

    @pl.when(count % 2 == 1)
    def _():
        use(even, count - 1)

    @pl.when((count % 2 == 0) & (count > 0))
    def _():
        make(odd, count - 1)
        use(even, count - 2)
        use(odd, count - 1)


def forward_pairs(count, q_ref, kband, vband, tile_of, place_of, even, odd, top, total, acc):
    def make(slot, i):
        scores = dot(kband[place_of[i]], q_ref[tile_of[i]], NT) * (SCALING * LOG2E)
        slot[0][...] = scores
        slot[1][...] = jnp.max(scores, axis=0, keepdims=True)

    def use(slot, i):
        tile = tile_of[i]
        before = top[tile]
        peak = jnp.maximum(before, slot[1][...])
        shrink = jnp.exp2(before - peak)
        raised = jnp.exp2(slot[0][...] - peak)
        top[tile] = peak
        total[tile] = shrink * total[tile] + jnp.sum(raised, axis=0, keepdims=True)
        acc[tile] = shrink * acc[tile] + dot(vband[place_of[i]], raised.astype(BF), TN)

    run_pairs(count, make, use, even, odd)


def forward_own_kernel(
    pattern_ref, q_ref, k_ref, v_ref, top, total, acc, tile_of, place_of, s0, s1, m0, m1
):
    count = build_pairs(pattern_ref, tile_of, place_of, (1,))
    top[...] = jnp.full(top.shape, -jnp.inf, F32)
    total[...] = jnp.zeros(total.shape, F32)
    acc[...] = jnp.zeros(acc.shape, F32)
    forward_pairs(
        count, q_ref, k_ref, v_ref, tile_of, place_of, (s0, m0), (s1, m1), top, total, acc
    )


def forward_halo_kernel(
    pattern_ref, q_ref, top_in, total_in, acc_in, ka_ref, kb_ref, va_ref, vb_ref, *rest
):
    att_ref, lse_ref, kband, vband, tile_of, place_of = rest[-13:-7]
    s0, s1, m0, m1, top, total, acc = rest[-7:]
    for band, refs in ((kband, (ka_ref, kb_ref)), (vband, (va_ref, vb_ref))):
        for i, ref in enumerate(refs):
            band[i * ROW_TILES : (i + 1) * ROW_TILES] = ref[...]
    count = build_pairs(pattern_ref, tile_of, place_of, (0, 2))
    top[...] = top_in[...]
    total[...] = total_in[...]
    acc[...] = acc_in[...]
    forward_pairs(
        count, q_ref, kband, vband, tile_of, place_of, (s0, m0), (s1, m1), top, total, acc
    )
    for tile in range(ROW_TILES):
        att_ref[tile] = (acc[tile] / total[tile]).astype(BF)
        lse_ref[tile] = top[tile] + jnp.log2(total[tile])


def backward_pairs(
    count, q_ref, back, att_ref, lse_ref, kband, vband, tile_of, place_of,
    even, odd, delta, dk, dv, dq,
):
    for tile in range(ROW_TILES):
        prod = back[tile].astype(F32) * att_ref[tile].astype(F32)
        delta[tile] = jnp.sum(prod, axis=0, keepdims=True)

    def make(slot, i):
        tile, place = tile_of[i], place_of[i]
        scores = dot(kband[place], q_ref[tile], NT) * (SCALING * LOG2E)
        prob = jnp.exp2(scores - lse_ref[tile])
        prob_grad = dot(vband[place], back[tile], NN)
        slot[0][...] = prob.astype(BF)
        slot[1][...] = (prob * (prob_grad - delta[tile])).astype(BF)

    def use(slot, i):
        tile, place = tile_of[i], place_of[i]
        dv[place] += dot(slot[0][...], back[tile], NT)
        dk[place] += dot(slot[1][...], q_ref[tile], NN)
        dq[tile] += dot(kband[place], slot[1][...], TN)

    run_pairs(count, make, use, even, odd)


def backward_edge(
    row, pattern_ref, q_ref, back_ref, att_ref, lse_ref, k_ref, v_ref,
    grads_ref, dq, tile_of, place_of, p0, p1, d0, d1, delta, dk, dv,
):
    count = build_pairs(pattern_ref, tile_of, place_of, (row,))
    dk[...] = jnp.zeros(dk.shape, F32)
    dv[...] = jnp.zeros(dv.shape, F32)
    backward_pairs(
        count, q_ref, back_ref, att_ref, lse_ref, k_ref, v_ref,
        tile_of, place_of, (p0, d0), (p1, d1), delta, dk, dv, dq,
    )
    grads_ref[0] = dk[...].astype(BF)
    grads_ref[1] = dv[...].astype(BF)


def backward_above_kernel(
    pattern_ref, q_ref, mine_ref, got_ref, att_ref, lse_ref, k_ref, v_ref,
    grads_ref, dq, back_ref, *scratch
):
    for tile in range(ROW_TILES):
        cols = pl.ds(tile * TILE, TILE)
        back_ref[tile] = (mine_ref[:, cols] + got_ref[:, cols].astype(F32)).astype(BF)
    dq[...] = jnp.zeros(dq.shape, F32)
    backward_edge(
        0, pattern_ref, q_ref, back_ref, att_ref, lse_ref, k_ref, v_ref, grads_ref, dq, *scratch
    )


def backward_below_kernel(
    pattern_ref, q_ref, back_ref, att_ref, lse_ref, k_ref, v_ref, dq_in,
    grads_ref, dq, zero_ref, *scratch
):
    zero_ref[...] = jnp.zeros(zero_ref.shape, F32)
    dq[...] = dq_in[...]
    backward_edge(
        2, pattern_ref, q_ref, back_ref, att_ref, lse_ref, k_ref, v_ref, grads_ref, dq, *scratch
    )


def backward_own_kernel(
    pattern_ref, q_ref, back_ref, att_ref, lse_ref, k_ref, v_ref, dq_in,
    dq_ref, dk, dv,
    tile_of, place_of, p0, p1, d0, d1, delta, dq,
):
    count = build_pairs(pattern_ref, tile_of, place_of, (1,))
    dk[...] = jnp.zeros(dk.shape, F32)
    dv[...] = jnp.zeros(dv.shape, F32)
    dq[...] = dq_in[...]
    backward_pairs(
        count, q_ref, back_ref, att_ref, lse_ref, k_ref, v_ref, tile_of, place_of,
        (p0, d0), (p1, d1), delta, dk, dv, dq,
    )
    for tile in range(ROW_TILES):
        dq_ref[tile] = (dq[tile] * SCALING).T.astype(BF)


def back_kernel(other_ref, mine_ref, grad_ref, sent_ref, kept_ref):
    sent_ref[...] = dot(other_ref[...], grad_ref[...], NN).astype(BF)
    kept_ref[...] = dot(mine_ref[...], grad_ref[...], NN)


def part_kernel(mine_ref, other_ref, att_ref, got_ref, early_ref, part_ref, weights, heads):
    weights[:HDIM] = mine_ref[...]
    weights[HDIM:] = other_ref[...]
    for tile in range(ROW_TILES):
        heads[:HDIM] = att_ref[tile]
        heads[HDIM:] = got_ref[tile]
        part_ref[:, tile * TILE : (tile + 1) * TILE] = dot(weights[...], heads[...], TN).astype(BF)


def weight_kernel(place_ref, grad_ref, att_ref, got_ref, early_ref, send_ref, keep_ref, heads, total):
    half, core = place_ref[0], place_ref[1]
    mine = pl.ds(pl.multiple_of(half * HDIM, HDIM), HDIM)
    other = pl.ds(pl.multiple_of((1 - half) * HDIM, HDIM), HDIM)
    for tile in range(ROW_TILES):
        cols = slice(tile * TILE, (tile + 1) * TILE)
        heads[mine, cols] = att_ref[tile]
        heads[other, cols] = got_ref[tile]
    total[...] = dot(grad_ref[...], heads[...], NT)
    rows = send_ref.shape[3]
    for low in range(2):
        for xh in range(2):
            chunk = low * 4 + xh * 2
            keep = pl.ds(pl.multiple_of((chunk + core) * rows, 8), rows)
            send = pl.ds(pl.multiple_of((chunk + 1 - core) * rows, 8), rows)
            for a in range(2):
                lanes = slice(a * HDIM, (a + 1) * HDIM)
                keep_ref[a, low, xh] = total[keep, lanes]
                send_ref[a, low, xh] = total[send, lanes].astype(BF)


VM = pl.BlockSpec(memory_space=pltpu.VMEM)
SM = pl.BlockSpec(memory_space=pltpu.SMEM)
BLOCK = (ROW_TILES, TILE, HDIM)
FLIP = (ROW_TILES, HDIM, TILE)
LINE = (ROW_TILES, 1, TILE)
HALO = (2 * ROW_TILES, TILE, HDIM)
PAIR_LISTS = [pltpu.SMEM((49,), jnp.int32), pltpu.SMEM((49,), jnp.int32)]
HALO_BAND = [pltpu.VMEM(HALO, BF), pltpu.VMEM(HALO, BF)]
SCORES = [pltpu.VMEM((TILE, TILE), F32)] * 2 + [pltpu.VMEM((1, TILE), F32)] * 2
TERMS = [pltpu.VMEM((TILE, TILE), BF)] * 4


def kernel_call(kernel, name, outs, in_specs, scratch, flops):
    return pl.pallas_call(
        kernel,
        name=name,
        out_shape=tuple(jax.ShapeDtypeStruct(shape, kind) for shape, kind in outs),
        in_specs=in_specs,
        out_specs=(VM,) * len(outs),
        scratch_shapes=scratch,
        compiler_params=pltpu.CompilerParams(vmem_limit_bytes=60 * 1024 * 1024),
        cost_estimate=pl.CostEstimate(
            flops=flops, bytes_accessed=4_000_000, transcendentals=3_000_000
        ),
    )


def forward_own(*args):
    return kernel_call(
        forward_own_kernel, "forward_own", [(LINE, F32), (LINE, F32), (FLIP, F32)],
        [SM, VM, VM, VM], PAIR_LISTS + SCORES, 3_000_000_000,
    )(*args)


def forward_halo(*args):
    state = [pltpu.VMEM(LINE, F32), pltpu.VMEM(LINE, F32), pltpu.VMEM(FLIP, F32)]
    return kernel_call(
        forward_halo_kernel, "forward_halo", [(FLIP, BF), (LINE, F32)],
        [SM] + [VM] * (len(args) - 1), HALO_BAND + PAIR_LISTS + SCORES + state,
        5_000_000_000,
    )(*args)


GRADS = (2,) + BLOCK
EDGE_SCRATCH = PAIR_LISTS + TERMS + [
    pltpu.VMEM(LINE, F32), pltpu.VMEM(BLOCK, F32), pltpu.VMEM(BLOCK, F32)
]


def backward_above(*args):
    return kernel_call(
        backward_above_kernel, "backward_above",
        [(GRADS, BF), (FLIP, F32), (FLIP, BF)], [SM] + [VM] * 7,
        EDGE_SCRATCH, 6_000_000_000,
    )(*args)


def backward_below(*args):
    return kernel_call(
        backward_below_kernel, "backward_below",
        [(GRADS, BF), (FLIP, F32), ((1, HDIM), F32)], [SM] + [VM] * 7, EDGE_SCRATCH, 6_000_000_000,
    )(*args)


def backward_own(*args):
    outs = [(BLOCK, BF), (BLOCK, F32), (BLOCK, F32)]
    return kernel_call(
        backward_own_kernel, "backward_own", outs, [SM] + [VM] * 7,
        PAIR_LISTS + TERMS + [pltpu.VMEM(LINE, F32), pltpu.VMEM(FLIP, F32)],
        6_000_000_000,
    )(*args)


def back_parts(w_other, w_mine, grad_half):
    shape = (w_mine.shape[0], grad_half.shape[1])
    return kernel_call(
        back_kernel, "back_parts", [(shape, BF), (shape, F32)], [VM] * 3, [], 2_000_000_000
    )(w_other, w_mine, grad_half)


def projected_part(*args):
    feats = args[0].shape[1]
    return kernel_call(
        part_kernel, "projected_part", [((feats, ROW_TILES * TILE), BF)], [VM] * 5,
        [pltpu.VMEM((2 * HDIM, feats), BF), pltpu.VMEM((2 * HDIM, TILE), BF)], 2_000_000_000,
    )(*args)[0]


def weight_parts(place, grad_half, att, att_other, early):
    feats, tokens = grad_half.shape
    shape = (2, 2, 2, feats // 8, HDIM)
    return kernel_call(
        weight_kernel, "weight_parts", [(shape, BF), (shape, F32)], [SM] + [VM] * 4,
        [pltpu.VMEM((2 * HDIM, tokens), BF), pltpu.VMEM((feats, 2 * HDIM), F32)],
        2_000_000_000,
    )(place, grad_half, att, att_other, early)


def shifted(block, distance):
    route = [(i - distance, i) for i in range(16) if 0 <= i - distance < 16]
    return lax.ppermute(block, ST, route)


def swapped(block):
    return lax.ppermute(block, "xl", [(0, 1), (1, 0)])


def halved(part, axis, dim, bit):
    send = lax.dynamic_index_in_dim(part, 1 - bit, dim, keepdims=False).astype(BF)
    keep = lax.dynamic_index_in_dim(part, bit, dim, keepdims=False)
    return keep, lax.ppermute(send, axis, [(0, 1), (1, 0)])


def body(queries, key_rows, value_rows, out_grad, proj_weight, pattern):
    half, y = lax.axis_index("xl"), lax.axis_index("y")
    tokens = queries.shape[1]
    q = queries.reshape(BLOCK)
    keys, values = key_rows.reshape(BLOCK), value_rows.reshape(BLOCK)
    above = shifted(keys, 1), shifted(values, 1)
    below = shifted(keys, -1), shifted(values, -1)
    place = jnp.stack((half, lax.axis_index("core"))).astype(jnp.int32)

    grad_half = lax.all_gather(out_grad[0].T, "z", axis=0, tiled=True)
    feats = grad_half.shape[0]
    w_mine = lax.dynamic_slice_in_dim(proj_weight, half * feats, feats, 1)
    w_other = swapped(lax.dynamic_slice_in_dim(proj_weight, (1 - half) * feats, feats, 1))

    own_state = forward_own(pattern, q, keys, values)
    att, lse = forward_halo(
        pattern, q, *own_state, above[0], below[0], above[1], below[1], w_other
    )
    att_other = swapped(att)

    back_sent, back_mine = back_parts(w_other, w_mine, grad_half)
    back_got = swapped(back_sent)

    part = projected_part(w_mine, w_other, att, att_other, back_sent)
    projected = lax.psum_scatter(part, "z", scatter_dimension=0, tiled=True)
    projected = projected.T[None]

    sent, kept = weight_parts(place, grad_half, att, att_other, back_got)
    got = lax.ppermute(sent, "core", [(0, 1), (1, 0)])
    kept, got = halved(kept + got.astype(F32), "xh", 2, lax.axis_index("xh"))

    up, dq, back = backward_above(pattern, q, back_mine, back_got, att, lse, *above)
    up = shifted(up, -1)
    down, dq, zero = backward_below(pattern, q, back, att, lse, *below, dq)
    down = shifted(down, 1)
    kept = (kept + got.astype(F32) + zero).astype(BF).reshape((4,) + kept.shape[2:])
    summed = 0.0
    for k in range(4):
        piece = lax.dynamic_index_in_dim(kept, y ^ k, 0, keepdims=False)
        route = [
            (h * 4 + i, (i ^ k) // 2 * 4 + 2 * h + (i ^ k) % 2) for h in range(2) for i in range(4)
        ]
        summed = summed + lax.ppermute(piece, ("xl", "y"), route).astype(F32)
    weight_grad = summed.T

    dq, dk, dv = backward_own(pattern, q, back, att, lse, keys, values, dq)

    shape = (1, tokens, HDIM)
    key_grad = SCALING * (dk + up[0].astype(F32) + down[0].astype(F32))
    value_grad = dv + up[1].astype(F32) + down[1].astype(F32)
    key_grad = key_grad.astype(BF).reshape(shape)
    value_grad = value_grad.astype(BF).reshape(shape)
    return projected, dq.reshape(shape), key_grad, value_grad, weight_grad


def solution(mesh):
    fine = Mesh(mesh.devices.reshape(2, 8, 4, 2, 2), ("xl", "z", "y", "xh", "core"))
    fsdp = ("xl", "z")
    rows = P(None, ST, fsdp)
    return jax.shard_map(
        body,
        mesh=fine,
        in_specs=(rows, rows, rows, rows, P(fsdp, None), P(ST, None)),
        out_specs=(rows, rows, rows, rows, P(fsdp, ST)),
        check_vma=False,
    )
```

```python
import functools

import jax
import jax.numpy as jnp
from jax import lax
from jax.experimental import pallas as pl
from jax.experimental.pallas import tpu as pltpu
from jax.sharding import Mesh
from jax.sharding import PartitionSpec as P

HDIM = 128
TILE = 384
TF = 2
TC = 2
ROW_TILES = TF * TC
BAND = 3 * ROW_TILES
SCALING = HDIM ** (-0.5)
LOG2E = 1.4426950408889634
BF = jnp.bfloat16
F32 = jnp.float32
ST = ("y", "xh", "core")
NT = (((1,), (1,)), ((), ()))
TN = (((0,), (0,)), ((), ()))
NN = (((1,), (0,)), ((), ()))


def dot(a, b, dims):
    return lax.dot_general(a, b, dims, preferred_element_type=F32)


def build_pairs(pattern_ref, tile_of, place_of, rows):
    count = jnp.int32(0)
    for tile in range(ROW_TILES):
        frame, col = tile // TC, tile % TC
        for at, row in enumerate(rows):
            for inner in range(ROW_TILES):
                slot = (inner // TC - frame + 1) * 9 + row * 3 + (inner % TC - col + 1)
                tile_of[count] = jnp.int32(tile)
                place_of[count] = jnp.int32(at * ROW_TILES + inner)
                count = count + (pattern_ref[tile, slot] >= 0).astype(jnp.int32)
    return count


def run_pairs(count, make, use, even, odd):
    make(even, 0)

    def step(j, carry):
        i = 2 * j
        make(odd, i + 1)
        use(even, i)
        make(even, i + 2)
        use(odd, i + 1)
        return carry

    lax.fori_loop(0, (count - 1) // 2, step, 0)

    @pl.when(count % 2 == 1)
    def _():
        use(even, count - 1)

    @pl.when(count % 2 == 0)
    def _():
        make(odd, count - 1)
        use(even, count - 2)
        use(odd, count - 1)


def fill_band(refs, kband, vband, sem):
    copies = []
    for i, ref in enumerate(refs):
        place = pl.ds(i * ROW_TILES, ROW_TILES)
        copies.append(pltpu.make_async_copy(ref.at[0], kband.at[place], sem.at[2 * i]))
        copies.append(pltpu.make_async_copy(ref.at[1], vband.at[place], sem.at[2 * i + 1]))
    for copy in copies:
        copy.start()
    return copies


def forward_pairs(count, q_ref, kband, vband, tile_of, place_of, even, odd, top, total, acc):
    def make(slot, i):
        scores = dot(kband[place_of[i]], q_ref[tile_of[i]], NT) * (SCALING * LOG2E)
        slot[0][...] = scores
        slot[1][...] = jnp.max(scores, axis=0, keepdims=True)

    def use(slot, i):
        tile = tile_of[i]
        before = top[tile]
        peak = jnp.maximum(before, slot[1][...])
        shrink = jnp.exp2(before - peak)
        raised = jnp.exp2(slot[0][...] - peak)
        top[tile] = peak
        total[tile] = shrink * total[tile] + jnp.sum(raised, axis=0, keepdims=True)
        acc[tile] = shrink * acc[tile] + dot(vband[place_of[i]], raised.astype(BF), TN)

    run_pairs(count, make, use, even, odd)


def forward_own_kernel(
    pattern_ref, q_ref, k_ref, v_ref, top, total, acc, tile_of, place_of, s0, s1, m0, m1
):
    count = build_pairs(pattern_ref, tile_of, place_of, (1,))
    top[...] = jnp.full(top.shape, -jnp.inf, F32)
    total[...] = jnp.zeros(total.shape, F32)
    acc[...] = jnp.zeros(acc.shape, F32)
    forward_pairs(
        count, q_ref, k_ref, v_ref, tile_of, place_of, (s0, m0), (s1, m1), top, total, acc
    )


def forward_halo_kernel(
    pattern_ref, q_ref, top_in, total_in, acc_in, above_ref, below_ref, early_ref,
    att_ref, flip_ref, lse_ref,
    kband, vband, tile_of, place_of, s0, s1, m0, m1, top, total, acc, sem,
):
    copies = fill_band((above_ref, below_ref), kband, vband, sem)
    count = build_pairs(pattern_ref, tile_of, place_of, (0, 2))
    top[...] = top_in[...]
    total[...] = total_in[...]
    acc[...] = acc_in[...]
    for copy in copies:
        copy.wait()
    forward_pairs(
        count, q_ref, kband, vband, tile_of, place_of, (s0, m0), (s1, m1), top, total, acc
    )
    for tile in range(ROW_TILES):
        attended = acc[tile] / total[tile]
        flip_ref[tile] = attended.astype(BF)
        att_ref[tile] = attended.T.astype(BF)
        lse_ref[tile] = top[tile] + jnp.log2(total[tile])


def backward_pairs(
    count, q_ref, back, att_ref, lse_ref, kband, vband, tile_of, place_of,
    even, odd, delta, dk, dv, dq,
):
    for tile in range(ROW_TILES):
        prod = back[tile].astype(F32) * att_ref[tile].astype(F32)
        delta[tile] = jnp.sum(prod, axis=0, keepdims=True)

    def make(slot, i):
        tile, place = tile_of[i], place_of[i]
        scores = dot(kband[place], q_ref[tile], NT) * (SCALING * LOG2E)
        prob = jnp.exp2(scores - lse_ref[tile])
        prob_grad = dot(vband[place], back[tile], NN)
        slot[0][...] = prob.astype(BF)
        slot[1][...] = (prob * (prob_grad - delta[tile])).astype(BF)

    def use(slot, i):
        tile, place = tile_of[i], place_of[i]
        dv[place] += dot(slot[0][...], back[tile], NT)
        dk[place] += dot(slot[1][...], q_ref[tile], NN)
        dq[tile] += dot(kband[place], slot[1][...], TN)

    run_pairs(count, make, use, even, odd)


def backward_halo_kernel(
    pattern_ref, q_ref, back_mine_ref, back_got_ref, att_ref, lse_ref, above_ref, below_ref,
    early_ref,
    up_ref, down_ref, dq, back_ref, zero_ref,
    kband, vband, tile_of, place_of, p0, p1, d0, d1, delta, dk, dv, sem,
):
    copies = fill_band((above_ref, below_ref), kband, vband, sem)
    count = build_pairs(pattern_ref, tile_of, place_of, (0, 2))
    dk[...] = jnp.zeros(dk.shape, F32)
    dv[...] = jnp.zeros(dv.shape, F32)
    dq[...] = jnp.zeros(dq.shape, F32)
    zero_ref[...] = jnp.zeros(zero_ref.shape, F32)
    for tile in range(ROW_TILES):
        cols = pl.ds(tile * TILE, TILE)
        back_ref[tile] = (back_mine_ref[:, cols] + back_got_ref[:, cols].astype(F32)).astype(BF)
    for copy in copies:
        copy.wait()
    backward_pairs(
        count, q_ref, back_ref, att_ref, lse_ref, kband, vband, tile_of, place_of,
        (p0, d0), (p1, d1), delta, dk, dv, dq,
    )
    for i in range(ROW_TILES):
        up_ref[0, i] = dk[i].astype(BF)
        up_ref[1, i] = dv[i].astype(BF)
        down_ref[0, i] = dk[ROW_TILES + i].astype(BF)
        down_ref[1, i] = dv[ROW_TILES + i].astype(BF)


def backward_own_kernel(
    pattern_ref, q_ref, back_ref, att_ref, lse_ref, k_ref, v_ref, dq_in, early_ref,
    dq_ref, dk, dv, zero_ref,
    tile_of, place_of, p0, p1, d0, d1, delta, dq,
):
    count = build_pairs(pattern_ref, tile_of, place_of, (1,))
    dk[...] = jnp.zeros(dk.shape, F32)
    dv[...] = jnp.zeros(dv.shape, F32)
    zero_ref[...] = jnp.zeros(zero_ref.shape, F32)
    dq[...] = dq_in[...]
    backward_pairs(
        count, q_ref, back_ref, att_ref, lse_ref, k_ref, v_ref, tile_of, place_of,
        (p0, d0), (p1, d1), delta, dk, dv, dq,
    )
    for tile in range(ROW_TILES):
        dq_ref[tile] = (dq[tile] * SCALING).T.astype(BF)


def part_kernel(mine_ref, other_ref, att_ref, got_ref, early_ref, part_ref, weights, heads):
    weights[:HDIM] = mine_ref[...]
    weights[HDIM:] = other_ref[...]
    heads[:, :HDIM] = att_ref[...]
    heads[:, HDIM:] = got_ref[...]
    for tile in range(ROW_TILES):
        cols = slice(tile * TILE, (tile + 1) * TILE)
        terms = dot(weights[...], heads[cols], (((0,), (1,)), ((), ())))
        part_ref[:, cols] = terms.astype(BF)


def weight_kernel(place_ref, grad_ref, att_ref, other_ref, early_ref, send_ref, keep_ref, heads, total):
    half, core = place_ref[0], place_ref[1]
    heads[:, pl.ds(pl.multiple_of(half * HDIM, HDIM), HDIM)] = att_ref[...]
    heads[:, pl.ds(pl.multiple_of((1 - half) * HDIM, HDIM), HDIM)] = other_ref[...]
    total[...] = dot(grad_ref[...], heads[...], NN)
    rows = send_ref.shape[3]
    for low in range(2):
        for xh in range(2):
            chunk = low * 4 + xh * 2
            mine = pl.ds(pl.multiple_of((chunk + core) * rows, 8), rows)
            yours = pl.ds(pl.multiple_of((chunk + 1 - core) * rows, 8), rows)
            for a in range(2):
                lanes = slice(a * HDIM, (a + 1) * HDIM)
                keep_ref[a, low, xh] = total[mine, lanes]
                send_ref[a, low, xh] = total[yours, lanes].astype(BF)


VM = pl.BlockSpec(memory_space=pltpu.VMEM)
SM = pl.BlockSpec(memory_space=pltpu.SMEM)
HB = pl.BlockSpec(memory_space=pltpu.HBM)
BLOCK = (ROW_TILES, TILE, HDIM)
FLIP = (ROW_TILES, HDIM, TILE)
LINE = (ROW_TILES, 1, TILE)
HALO = (2 * ROW_TILES, TILE, HDIM)
PAIR_LISTS = [pltpu.SMEM((49,), jnp.int32), pltpu.SMEM((49,), jnp.int32)]
HALO_BAND = [pltpu.VMEM(HALO, BF), pltpu.VMEM(HALO, BF)]
SCORES = [pltpu.VMEM((TILE, TILE), F32)] * 2 + [pltpu.VMEM((1, TILE), F32)] * 2
TERMS = [pltpu.VMEM((TILE, TILE), BF)] * 4
DMA_SEMS = pltpu.SemaphoreType.DMA((4,))


def kernel_call(kernel, name, outs, in_specs, scratch, flops):
    return pl.pallas_call(
        kernel,
        name=name,
        out_shape=tuple(jax.ShapeDtypeStruct(shape, kind) for shape, kind in outs),
        in_specs=in_specs,
        out_specs=(VM,) * len(outs),
        scratch_shapes=scratch,
        compiler_params=pltpu.CompilerParams(vmem_limit_bytes=32 * 1024 * 1024),
        cost_estimate=pl.CostEstimate(
            flops=flops, bytes_accessed=4_000_000, transcendentals=3_000_000
        ),
    )


def forward_own(*args):
    return kernel_call(
        forward_own_kernel, "forward_own", [(LINE, F32), (LINE, F32), (FLIP, F32)],
        [SM, VM, VM, VM], PAIR_LISTS + SCORES, 3_000_000_000,
    )(*args)


def forward_halo(*args):
    state = [pltpu.VMEM(LINE, F32), pltpu.VMEM(LINE, F32), pltpu.VMEM(FLIP, F32)]
    return kernel_call(
        forward_halo_kernel, "forward_halo", [(BLOCK, BF), (FLIP, BF), (LINE, F32)],
        [SM] + [VM] * 4 + [HB] * 3, HALO_BAND + PAIR_LISTS + SCORES + state + [DMA_SEMS],
        5_000_000_000,
    )(*args)


def backward_halo(*args):
    outs = [((2,) + BLOCK, BF), ((2,) + BLOCK, BF), (FLIP, F32), (FLIP, BF), ((1, HDIM), F32)]
    return kernel_call(
        backward_halo_kernel, "backward_halo", outs, [SM] + [VM] * 5 + [HB] * 3,
        HALO_BAND + PAIR_LISTS + TERMS
        + [pltpu.VMEM(LINE, F32), pltpu.VMEM(HALO, F32), pltpu.VMEM(HALO, F32), DMA_SEMS],
        12_000_000_000,
    )(*args)


def backward_own(*args):
    outs = [(BLOCK, BF), (BLOCK, F32), (BLOCK, F32), ((1, HDIM), F32)]
    return kernel_call(
        backward_own_kernel, "backward_own", outs, [SM] + [VM] * 7 + [HB],
        PAIR_LISTS + TERMS + [pltpu.VMEM(LINE, F32), pltpu.VMEM(FLIP, F32)],
        6_000_000_000,
    )(*args)


def projected_part(w_mine, *args):
    feats, tokens = w_mine.shape[1], ROW_TILES * TILE
    return kernel_call(
        part_kernel, "projected_part", [((feats, tokens), BF)], [VM] * 4 + [HB],
        [pltpu.VMEM((2 * HDIM, feats), BF), pltpu.VMEM((tokens, 2 * HDIM), BF)], 2_000_000_000,
    )(w_mine, *args)[0]


def weight_parts(place, grad_half, att, att_other, early):
    feats, tokens = grad_half.shape
    shape = (2, 2, 2, feats // 8, HDIM)
    return kernel_call(
        weight_kernel, "weight_parts", [(shape, BF), (shape, F32)], [SM] + [VM] * 3 + [HB],
        [pltpu.VMEM((tokens, 2 * HDIM), BF), pltpu.VMEM((feats, 2 * HDIM), F32)],
        2_000_000_000,
    )(place, grad_half, att, att_other, early)


def shifted(block, distance):
    route = [(i - distance, i) for i in range(16) if 0 <= i - distance < 16]
    return lax.ppermute(block, ST, route)


def swapped(block):
    return lax.ppermute(block, "xl", [(0, 1), (1, 0)])


def halved(part, axis, distance, size, dim, bit):
    route = [(i, i ^ distance) for i in range(size)]
    send = lax.dynamic_index_in_dim(part, 1 - bit, dim, keepdims=False).astype(BF)
    keep = lax.dynamic_index_in_dim(part, bit, dim, keepdims=False)
    return keep, lax.ppermute(send, axis, route)


def body(queries, key_rows, value_rows, out_grad, proj_weight, pattern):
    half, y = lax.axis_index("xl"), lax.axis_index("y")
    tokens = queries.shape[1]
    place = jnp.stack((half, lax.axis_index("core"))).astype(jnp.int32)
    places = lax.axis_size("z")
    q = queries.reshape(BLOCK)
    keys, values = key_rows.reshape(BLOCK), value_rows.reshape(BLOCK)
    kv = jnp.stack((keys, values))
    above, below = shifted(kv, 1), shifted(kv, -1)

    block = out_grad[0].T
    feats = places * block.shape[0]
    copies = jnp.broadcast_to(block, (places,) + block.shape)
    grad_half = lax.all_to_all(copies, "z", 0, 0, tiled=True).reshape(feats, tokens)
    w_mine = lax.dynamic_slice_in_dim(proj_weight, half * feats, feats, 1)
    w_other = swapped(lax.dynamic_slice_in_dim(proj_weight, (1 - half) * feats, feats, 1))

    own_state = forward_own(pattern, q, keys, values)
    attended, att_flip, lse = forward_halo(pattern, q, *own_state, above, below, w_other)
    att = attended.reshape(tokens, HDIM)
    att_other = swapped(att)

    back_sent = dot(w_other, grad_half, NN).astype(BF)
    back_got = swapped(back_sent)
    back_mine = dot(w_mine, grad_half, NN)

    part = projected_part(w_mine, w_other, att, att_other, back_sent)
    parts = lax.all_to_all(part.reshape((places,) + block.shape), "z", 0, 0, tiled=True)
    projected = jnp.sum(parts.astype(F32), axis=0).astype(BF).T[None]

    sent, kept = weight_parts(place, grad_half, att, att_other, back_sent)
    got = lax.ppermute(sent, "core", [(0, 1), (1, 0)])
    kept, got = halved(kept + got.astype(F32), "xh", 1, 2, 2, lax.axis_index("xh"))

    up, down, dq_part, back, _ = backward_halo(
        pattern, q, back_mine, back_got, att_flip, lse, above, below, sent
    )
    up, down = shifted(up, -1), shifted(down, 1)
    dq, dk, dv, zero = backward_own(pattern, q, back, att_flip, lse, keys, values, dq_part, kept)

    kept = (kept + got.astype(F32) + zero).astype(BF).reshape((4,) + kept.shape[2:])
    summed = 0.0
    for k in range(4):
        piece = lax.dynamic_index_in_dim(kept, y ^ k, 0, keepdims=False)
        route = [
            (h * 4 + i, (i ^ k) // 2 * 4 + 2 * h + (i ^ k) % 2) for h in range(2) for i in range(4)
        ]
        summed = summed + lax.ppermute(piece, ("xl", "y"), route).astype(F32)
    weight_grad = summed.T

    shape = (1, tokens, HDIM)
    key_grad = SCALING * (dk + up[0].astype(F32) + down[0].astype(F32))
    value_grad = dv + up[1].astype(F32) + down[1].astype(F32)
    key_grad = key_grad.astype(BF).reshape(shape)
    value_grad = value_grad.astype(BF).reshape(shape)
    return projected, dq.reshape(shape), key_grad, value_grad, weight_grad


def solution(mesh):
    fine = Mesh(mesh.devices.reshape(2, 8, 4, 2, 2), ("xl", "z", "y", "xh", "core"))
    fsdp = ("xl", "z")
    rows = P(None, ST, fsdp)
    return jax.shard_map(
        body,
        mesh=fine,
        in_specs=(rows, rows, rows, rows, P(fsdp, None), P(ST, None)),
        out_specs=(rows, rows, rows, rows, P(fsdp, ST)),
        check_vma=False,
    )
```

```python
import functools

import jax
import jax.numpy as jnp
from jax import lax
from jax.experimental import pallas as pl
from jax.experimental.pallas import tpu as pltpu
from jax.sharding import Mesh
from jax.sharding import PartitionSpec as P

HDIM = 128
TILE = 384
TF = 2
TC = 2
ROW_TILES = TF * TC
BAND = 3 * ROW_TILES
SCALING = HDIM ** (-0.5)
LOG2E = 1.4426950408889634
BF = jnp.bfloat16
F32 = jnp.float32
ST = ("y", "xh", "core")
NT = (((1,), (1,)), ((), ()))
TN = (((0,), (0,)), ((), ()))
NN = (((1,), (0,)), ((), ()))


def dot(a, b, dims):
    return lax.dot_general(a, b, dims, preferred_element_type=F32)


def build_pairs(pattern_ref, tile_of, place_of, rows):
    count = jnp.int32(0)
    for tile in range(ROW_TILES):
        frame, col = tile // TC, tile % TC
        for at, row in enumerate(rows):
            for inner in range(ROW_TILES):
                slot = (inner // TC - frame + 1) * 9 + row * 3 + (inner % TC - col + 1)
                tile_of[count] = jnp.int32(tile)
                place_of[count] = jnp.int32(at * ROW_TILES + inner)
                count = count + (pattern_ref[tile, slot] >= 0).astype(jnp.int32)
    return count


def run_pairs(count, make, use, even, odd):
    make(even, 0)

    def step(j, carry):
        i = 2 * j
        make(odd, i + 1)
        use(even, i)
        make(even, i + 2)
        use(odd, i + 1)
        return carry

    lax.fori_loop(0, (count - 1) // 2, step, 0)

    @pl.when(count % 2 == 1)
    def _():
        use(even, count - 1)

    @pl.when(count % 2 == 0)
    def _():
        make(odd, count - 1)
        use(even, count - 2)
        use(odd, count - 1)


def fill_band(refs, kband, vband, sem):
    copies = []
    for i, ref in enumerate(refs):
        place = pl.ds(i * ROW_TILES, ROW_TILES)
        copies.append(pltpu.make_async_copy(ref.at[0], kband.at[place], sem.at[2 * i]))
        copies.append(pltpu.make_async_copy(ref.at[1], vband.at[place], sem.at[2 * i + 1]))
    for copy in copies:
        copy.start()
    return copies


def forward_pairs(count, q_ref, kband, vband, tile_of, place_of, even, odd, top, total, acc):
    def make(slot, i):
        scores = dot(kband[place_of[i]], q_ref[tile_of[i]], NT) * (SCALING * LOG2E)
        slot[0][...] = scores
        slot[1][...] = jnp.max(scores, axis=0, keepdims=True)

    def use(slot, i):
        tile = tile_of[i]
        before = top[tile]
        peak = jnp.maximum(before, slot[1][...])
        shrink = jnp.exp2(before - peak)
        raised = jnp.exp2(slot[0][...] - peak)
        top[tile] = peak
        total[tile] = shrink * total[tile] + jnp.sum(raised, axis=0, keepdims=True)
        acc[tile] = shrink * acc[tile] + dot(vband[place_of[i]], raised.astype(BF), TN)

    run_pairs(count, make, use, even, odd)


def forward_own_kernel(
    pattern_ref, q_ref, k_ref, v_ref, e0, e1,
    top, total, acc, tile_of, place_of, s0, s1, m0, m1,
):
    count = build_pairs(pattern_ref, tile_of, place_of, (1,))
    top[...] = jnp.full(top.shape, -jnp.inf, F32)
    total[...] = jnp.zeros(total.shape, F32)
    acc[...] = jnp.zeros(acc.shape, F32)
    forward_pairs(
        count, q_ref, k_ref, v_ref, tile_of, place_of, (s0, m0), (s1, m1), top, total, acc
    )


def forward_halo_kernel(
    pattern_ref, q_ref, top_in, total_in, acc_in, above_ref, below_ref, early_ref,
    att_ref, flip_ref, lse_ref,
    kband, vband, tile_of, place_of, s0, s1, m0, m1, top, total, acc, sem,
):
    copies = fill_band((above_ref, below_ref), kband, vband, sem)
    count = build_pairs(pattern_ref, tile_of, place_of, (0, 2))
    top[...] = top_in[...]
    total[...] = total_in[...]
    acc[...] = acc_in[...]
    for copy in copies:
        copy.wait()
    forward_pairs(
        count, q_ref, kband, vband, tile_of, place_of, (s0, m0), (s1, m1), top, total, acc
    )
    for tile in range(ROW_TILES):
        attended = acc[tile] / total[tile]
        flip_ref[tile] = attended.astype(BF)
        att_ref[tile] = attended.T.astype(BF)
        lse_ref[tile] = top[tile] + jnp.log2(total[tile])


def backward_pairs(
    count, q_ref, back, att_ref, lse_ref, kband, vband, tile_of, place_of,
    even, odd, delta, dk, dv, dq,
):
    for tile in range(ROW_TILES):
        prod = back[tile].astype(F32) * att_ref[tile].astype(F32)
        delta[tile] = jnp.sum(prod, axis=0, keepdims=True)

    def make(slot, i):
        tile, place = tile_of[i], place_of[i]
        scores = dot(kband[place], q_ref[tile], NT) * (SCALING * LOG2E)
        prob = jnp.exp2(scores - lse_ref[tile])
        prob_grad = dot(vband[place], back[tile], NN)
        slot[0][...] = prob.astype(BF)
        slot[1][...] = (prob * (prob_grad - delta[tile])).astype(BF)

    def use(slot, i):
        tile, place = tile_of[i], place_of[i]
        dv[place] += dot(slot[0][...], back[tile], NT)
        dk[place] += dot(slot[1][...], q_ref[tile], NN)
        dq[tile] += dot(kband[place], slot[1][...], TN)

    run_pairs(count, make, use, even, odd)


def backward_halo_kernel(
    pattern_ref, q_ref, back_mine_ref, back_got_ref, att_ref, lse_ref, above_ref, below_ref,
    up_ref, down_ref, dq, back_ref, zero_ref,
    kband, vband, tile_of, place_of, p0, p1, d0, d1, delta, dk, dv, sem,
):
    copies = fill_band((above_ref, below_ref), kband, vband, sem)
    count = build_pairs(pattern_ref, tile_of, place_of, (0, 2))
    dk[...] = jnp.zeros(dk.shape, F32)
    dv[...] = jnp.zeros(dv.shape, F32)
    dq[...] = jnp.zeros(dq.shape, F32)
    zero_ref[...] = jnp.zeros(zero_ref.shape, F32)
    for tile in range(ROW_TILES):
        cols = pl.ds(tile * TILE, TILE)
        back_ref[tile] = (back_mine_ref[:, cols] + back_got_ref[:, cols].astype(F32)).astype(BF)
    for copy in copies:
        copy.wait()
    backward_pairs(
        count, q_ref, back_ref, att_ref, lse_ref, kband, vband, tile_of, place_of,
        (p0, d0), (p1, d1), delta, dk, dv, dq,
    )
    for i in range(ROW_TILES):
        up_ref[0, i] = dk[i].astype(BF)
        up_ref[1, i] = dv[i].astype(BF)
        down_ref[0, i] = dk[ROW_TILES + i].astype(BF)
        down_ref[1, i] = dv[ROW_TILES + i].astype(BF)


def backward_own_kernel(
    pattern_ref, q_ref, back_ref, att_ref, lse_ref, k_ref, v_ref, dq_in, up_ref, down_ref,
    dq_ref, dk_ref, dv_ref, zero_ref,
    tile_of, place_of, p0, p1, d0, d1, delta, dq, dk, dv,
):
    count = build_pairs(pattern_ref, tile_of, place_of, (1,))
    dk[...] = up_ref[0].astype(F32) + down_ref[0].astype(F32)
    dv[...] = up_ref[1].astype(F32) + down_ref[1].astype(F32)
    zero_ref[...] = jnp.zeros(zero_ref.shape, F32)
    dq[...] = dq_in[...]
    backward_pairs(
        count, q_ref, back_ref, att_ref, lse_ref, k_ref, v_ref, tile_of, place_of,
        (p0, d0), (p1, d1), delta, dk, dv, dq,
    )
    for tile in range(ROW_TILES):
        dq_ref[tile] = (dq[tile] * SCALING).T.astype(BF)
        dk_ref[tile] = (dk[tile] * SCALING).astype(BF)
        dv_ref[tile] = dv[tile].astype(BF)


def back_kernel(place_ref, other_ref, mine_ref, *refs):
    blocks, (grad, sent_ref, kept_ref) = refs[:-3], refs[-3:]
    rows, tokens = blocks[0].shape

    def at(offset):
        source = lax.rem(place_ref[2] + offset + 8, 8)
        return pl.ds(pl.multiple_of(source * rows, 32), rows)

    for offset, block in zip(RING, blocks):
        grad[at(offset)] = block[...]
    grad[at(4), : tokens // 2] = blocks[-2][...]
    grad[at(4), tokens // 2 :] = blocks[-1][...]
    sent_ref[...] = dot(other_ref[...], grad[...], NN).astype(BF)
    kept_ref[...] = dot(mine_ref[...], grad[...], NN)


def part_kernel(place_ref, mine_ref, other_ref, att_ref, got_ref, early_ref, *refs):
    blocks, (weights, heads, total) = refs[:-3], refs[-3:]
    rows, tokens = blocks[0].shape
    weights[:HDIM] = mine_ref[...]
    weights[HDIM:] = other_ref[...]
    heads[:, :HDIM] = att_ref[...]
    heads[:, HDIM:] = got_ref[...]
    for tile in range(ROW_TILES):
        cols = slice(tile * TILE, (tile + 1) * TILE)
        terms = dot(weights[...], heads[cols], (((0,), (1,)), ((), ())))
        total[:, cols] = terms.astype(BF)

    def at(offset):
        target = lax.rem(place_ref[2] + offset + 8, 8)
        return pl.ds(pl.multiple_of(target * rows, 32), rows)

    for offset, block in zip(RING, blocks):
        block[...] = total[at(offset)]
    blocks[-2][...] = total[at(4), : tokens // 2]
    blocks[-1][...] = total[at(4), tokens // 2 :]


def weight_kernel(place_ref, grad_ref, att_ref, other_ref, early_ref, send_ref, keep_ref, heads, total):
    half, core = place_ref[0], place_ref[1]
    heads[:, pl.ds(pl.multiple_of(half * HDIM, HDIM), HDIM)] = att_ref[...]
    heads[:, pl.ds(pl.multiple_of((1 - half) * HDIM, HDIM), HDIM)] = other_ref[...]
    total[...] = dot(grad_ref[...], heads[...], NN)
    rows = send_ref.shape[3]
    for low in range(2):
        for xh in range(2):
            chunk = low * 4 + xh * 2
            mine = pl.ds(pl.multiple_of((chunk + core) * rows, 8), rows)
            yours = pl.ds(pl.multiple_of((chunk + 1 - core) * rows, 8), rows)
            for a in range(2):
                lanes = slice(a * HDIM, (a + 1) * HDIM)
                keep_ref[a, low, xh] = total[mine, lanes]
                send_ref[a, low, xh] = total[yours, lanes].astype(BF)


VM = pl.BlockSpec(memory_space=pltpu.VMEM)
SM = pl.BlockSpec(memory_space=pltpu.SMEM)
HB = pl.BlockSpec(memory_space=pltpu.HBM)
ANY = pl.BlockSpec(memory_space=pl.ANY)
BLOCK = (ROW_TILES, TILE, HDIM)
FLIP = (ROW_TILES, HDIM, TILE)
LINE = (ROW_TILES, 1, TILE)
RING = (0, -1, 1, -2, 2, -3, 3)
HALO = (2 * ROW_TILES, TILE, HDIM)
PAIR_LISTS = [pltpu.SMEM((49,), jnp.int32), pltpu.SMEM((49,), jnp.int32)]
HALO_BAND = [pltpu.VMEM(HALO, BF), pltpu.VMEM(HALO, BF)]
SCORES = [pltpu.VMEM((TILE, TILE), F32)] * 2 + [pltpu.VMEM((1, TILE), F32)] * 2
TERMS = [pltpu.VMEM((TILE, TILE), BF)] * 4
DMA_SEMS = pltpu.SemaphoreType.DMA((4,))


def kernel_call(kernel, name, outs, in_specs, scratch, flops):
    return pl.pallas_call(
        kernel,
        name=name,
        out_shape=tuple(jax.ShapeDtypeStruct(shape, kind) for shape, kind in outs),
        in_specs=in_specs,
        out_specs=(VM,) * len(outs),
        scratch_shapes=scratch,
        compiler_params=pltpu.CompilerParams(vmem_limit_bytes=32 * 1024 * 1024),
        cost_estimate=pl.CostEstimate(
            flops=flops, bytes_accessed=4_000_000, transcendentals=3_000_000
        ),
    )


def forward_own(*args):
    return kernel_call(
        forward_own_kernel, "forward_own", [(LINE, F32), (LINE, F32), (FLIP, F32)],
        [SM, VM, VM, VM, ANY, ANY], PAIR_LISTS + SCORES, 3_000_000_000,
    )(*args)


def forward_halo(*args):
    state = [pltpu.VMEM(LINE, F32), pltpu.VMEM(LINE, F32), pltpu.VMEM(FLIP, F32)]
    return kernel_call(
        forward_halo_kernel, "forward_halo", [(BLOCK, BF), (FLIP, BF), (LINE, F32)],
        [SM] + [VM] * 4 + [HB] * 2 + [ANY], HALO_BAND + PAIR_LISTS + SCORES + state + [DMA_SEMS],
        5_000_000_000,
    )(*args)


def backward_halo(*args):
    outs = [((2,) + BLOCK, BF), ((2,) + BLOCK, BF), (FLIP, F32), (FLIP, BF), ((1, HDIM), F32)]
    return kernel_call(
        backward_halo_kernel, "backward_halo", outs, [SM] + [VM] * 5 + [HB] * 2,
        HALO_BAND + PAIR_LISTS + TERMS
        + [pltpu.VMEM(LINE, F32), pltpu.VMEM(HALO, F32), pltpu.VMEM(HALO, F32), DMA_SEMS],
        12_000_000_000,
    )(*args)


def backward_own(*args):
    outs = [(BLOCK, BF), (BLOCK, BF), (BLOCK, BF), ((1, HDIM), F32)]
    return kernel_call(
        backward_own_kernel, "backward_own", outs, [SM] + [VM] * 9,
        PAIR_LISTS + TERMS
        + [pltpu.VMEM(LINE, F32), pltpu.VMEM(FLIP, F32)] + [pltpu.VMEM(BLOCK, F32)] * 2,
        6_000_000_000,
    )(*args)


def back_parts(place, w_other, w_mine, blocks):
    heads, feats = w_mine.shape
    tokens = blocks[0].shape[1]
    outs = [((feats, tokens), BF), ((heads, tokens), BF), ((heads, tokens), F32)]
    return kernel_call(
        back_kernel, "back_parts", outs, [SM] + [VM] * (2 + len(blocks)), [], 2_000_000_000
    )(place, w_other, w_mine, *blocks)


def projected_parts(place, w_mine, *args):
    feats, tokens = w_mine.shape[1], ROW_TILES * TILE
    outs = [((feats // 8, tokens), BF)] * 7 + [((feats // 8, tokens // 2), BF)] * 2
    return kernel_call(
        part_kernel, "projected_parts", outs, [SM] + [VM] * 4 + [ANY],
        [
            pltpu.VMEM((2 * HDIM, feats), BF),
            pltpu.VMEM((tokens, 2 * HDIM), BF),
            pltpu.VMEM((feats, tokens), BF),
        ],
        2_000_000_000,
    )(place, w_mine, *args)


def weight_parts(place, grad_half, att, att_other, early):
    feats, tokens = grad_half.shape
    shape = (2, 2, 2, feats // 8, HDIM)
    return kernel_call(
        weight_kernel, "weight_parts", [(shape, BF), (shape, F32)], [SM] + [VM] * 3 + [HB],
        [pltpu.VMEM((tokens, 2 * HDIM), BF), pltpu.VMEM((feats, 2 * HDIM), F32)],
        2_000_000_000,
    )(place, grad_half, att, att_other, early)


def shifted(block, distance):
    route = [(i - distance, i) for i in range(16) if 0 <= i - distance < 16]
    return lax.ppermute(block, ST, route)


def swapped(block):
    return lax.ppermute(block, "xl", [(0, 1), (1, 0)])


def halved(part, axis, distance, size, dim, bit):
    route = [(i, i ^ distance) for i in range(size)]
    send = lax.dynamic_index_in_dim(part, 1 - bit, dim, keepdims=False).astype(BF)
    keep = lax.dynamic_index_in_dim(part, bit, dim, keepdims=False)
    return keep, lax.ppermute(send, axis, route)


def ring_gathered(block):
    size = lax.axis_size("z")
    onward = [(i, (i + 1) % size) for i in range(size)]
    backward = [(j, i) for i, j in onward]
    right = left = block
    got = [block]
    for _ in range(size // 2 - 1):
        right, left = lax.ppermute(right, "z", onward), lax.ppermute(left, "z", backward)
        got += [right, left]
    middle = block.shape[1] // 2
    far = [lax.ppermute(right[:, :middle], "z", onward), lax.ppermute(left[:, middle:], "z", backward)]
    return got + far


def ring_summed(parts, late):
    size = lax.axis_size("z")
    onward = [(i, (i + 1) % size) for i in range(size)]
    backward = [(j, i) for i, j in onward]
    middle = parts[-1].shape[1]
    right = lax.ppermute(parts[-2], "z", onward).astype(F32)
    left = lax.ppermute(parts[-1], "z", backward).astype(F32)
    by_offset = {offset: part.astype(F32) for offset, part in zip(RING, parts)}
    last = size // 2 - 1
    right = jnp.concatenate((by_offset[last][:, :middle] + right, by_offset[last][:, middle:]), axis=1)
    left = jnp.concatenate((by_offset[-last][:, :middle], by_offset[-last][:, middle:] + left), axis=1)
    for offset in range(last - 1, -1, -1):
        if offset == 0:
            right, left = right + late, left + late
        right = lax.ppermute(right.astype(BF), "z", onward).astype(F32)
        left = lax.ppermute(left.astype(BF), "z", backward).astype(F32)
        if offset:
            right, left = right + by_offset[offset], left + by_offset[-offset]
    return right + left + by_offset[0]


def body(queries, key_rows, value_rows, out_grad, proj_weight, pattern):
    half, y = lax.axis_index("xl"), lax.axis_index("y")
    tokens = queries.shape[1]
    place = jnp.stack((half, lax.axis_index("core"), lax.axis_index("z"))).astype(jnp.int32)
    places = lax.axis_size("z")
    q = queries.reshape(BLOCK)
    keys, values = key_rows.reshape(BLOCK), value_rows.reshape(BLOCK)
    kv = jnp.stack((keys, values))
    above, below = shifted(kv, 1), shifted(kv, -1)

    block = out_grad[0].T
    feats = places * block.shape[0]
    blocks = ring_gathered(block)
    w_mine = lax.dynamic_slice_in_dim(proj_weight, half * feats, feats, 1)
    w_other = swapped(lax.dynamic_slice_in_dim(proj_weight, (1 - half) * feats, feats, 1))

    grad_half, back_sent, back_mine = back_parts(place, w_other, w_mine, blocks)
    back_got = swapped(back_sent)

    own_state = forward_own(pattern, q, keys, values, above, below)
    attended, att_flip, lse = forward_halo(pattern, q, *own_state, above, below, back_sent)
    att = attended.reshape(tokens, HDIM)
    att_other = swapped(att)

    up, down, dq_part, back, zero = backward_halo(
        pattern, q, back_mine, back_got, att_flip, lse, above, below
    )
    up, down = shifted(up, -1), shifted(down, 1)
    dq, dk, dv, late = backward_own(
        pattern, q, back, att_flip, lse, keys, values, dq_part, up, down
    )

    parts = projected_parts(place, w_mine, w_other, att, att_other, zero)
    projected = ring_summed(parts, late[:, :1]).astype(BF).T[None]

    sent, kept = weight_parts(place, grad_half, att, att_other, zero)
    got = lax.ppermute(sent, "core", [(0, 1), (1, 0)])
    kept, got = halved(kept + got.astype(F32), "xh", 1, 2, 2, lax.axis_index("xh"))

    kept = (kept + got.astype(F32)).astype(BF).reshape((4,) + kept.shape[2:])
    summed = 0.0
    for k in range(4):
        piece = lax.dynamic_index_in_dim(kept, y ^ k, 0, keepdims=False)
        route = [
            (h * 4 + i, (i ^ k) // 2 * 4 + 2 * h + (i ^ k) % 2) for h in range(2) for i in range(4)
        ]
        summed = summed + lax.ppermute(piece, ("xl", "y"), route).astype(F32)
    weight_grad = summed.T

    shape = (1, tokens, HDIM)
    return projected, dq.reshape(shape), dk.reshape(shape), dv.reshape(shape), weight_grad


def solution(mesh):
    fine = Mesh(mesh.devices.reshape(2, 8, 4, 2, 2), ("xl", "z", "y", "xh", "core"))
    fsdp = ("xl", "z")
    rows = P(None, ST, fsdp)
    return jax.shard_map(
        body,
        mesh=fine,
        in_specs=(rows, rows, rows, rows, P(fsdp, None), P(ST, None)),
        out_specs=(rows, rows, rows, rows, P(fsdp, ST)),
        check_vma=False,
    )
```

```python
import functools

import jax
import jax.numpy as jnp
from jax import lax
from jax.experimental import pallas as pl
from jax.experimental.pallas import tpu as pltpu
from jax.sharding import Mesh
from jax.sharding import PartitionSpec as P

HDIM = 128
TILE = 384
TF = 2
TC = 2
ROW_TILES = TF * TC
BAND = 3 * ROW_TILES
SCALING = HDIM ** (-0.5)
LOG2E = 1.4426950408889634
BF = jnp.bfloat16
F32 = jnp.float32
ST = ("y", "xh", "core")
NT = (((1,), (1,)), ((), ()))
TN = (((0,), (0,)), ((), ()))
NN = (((1,), (0,)), ((), ()))


def dot(a, b, dims):
    return lax.dot_general(a, b, dims, preferred_element_type=F32)


def build_pairs(pattern_ref, tile_of, place_of, rows):
    count = jnp.int32(0)
    for tile in range(ROW_TILES):
        frame, col = tile // TC, tile % TC
        for at, row in enumerate(rows):
            for inner in range(ROW_TILES):
                slot = (inner // TC - frame + 1) * 9 + row * 3 + (inner % TC - col + 1)
                tile_of[count] = jnp.int32(tile)
                place_of[count] = jnp.int32(at * ROW_TILES + inner)
                count = count + (pattern_ref[tile, slot] >= 0).astype(jnp.int32)
    return count


def run_pairs(count, make, use, even, odd):
    make(even, 0)

    def step(j, carry):
        i = 2 * j
        make(odd, i + 1)
        use(even, i)
        make(even, i + 2)
        use(odd, i + 1)
        return carry

    lax.fori_loop(0, (count - 1) // 2, step, 0)

    @pl.when(count % 2 == 1)
    def _():
        use(even, count - 1)

    @pl.when(count % 2 == 0)
    def _():
        make(odd, count - 1)
        use(even, count - 2)
        use(odd, count - 1)


def fill_band(refs, kband, vband, sem):
    copies = []
    for i, ref in enumerate(refs):
        place = pl.ds(i * ROW_TILES, ROW_TILES)
        copies.append(pltpu.make_async_copy(ref.at[0], kband.at[place], sem.at[2 * i]))
        copies.append(pltpu.make_async_copy(ref.at[1], vband.at[place], sem.at[2 * i + 1]))
    for copy in copies:
        copy.start()
    return copies


def forward_pairs(count, q_ref, kband, vband, tile_of, place_of, even, odd, top, total, acc):
    def make(slot, i):
        scores = dot(kband[place_of[i]], q_ref[tile_of[i]], NT) * (SCALING * LOG2E)
        slot[0][...] = scores
        slot[1][...] = jnp.max(scores, axis=0, keepdims=True)

    def use(slot, i):
        tile = tile_of[i]
        before = top[tile]
        peak = jnp.maximum(before, slot[1][...])
        shrink = jnp.exp2(before - peak)
        raised = jnp.exp2(slot[0][...] - peak)
        top[tile] = peak
        total[tile] = shrink * total[tile] + jnp.sum(raised, axis=0, keepdims=True)
        acc[tile] = shrink * acc[tile] + dot(vband[place_of[i]], raised.astype(BF), TN)

    run_pairs(count, make, use, even, odd)


def forward_own_kernel(
    pattern_ref, q_ref, k_ref, v_ref, e0, e1,
    top, total, acc, tile_of, place_of, s0, s1, m0, m1,
):
    count = build_pairs(pattern_ref, tile_of, place_of, (1,))
    top[...] = jnp.full(top.shape, -jnp.inf, F32)
    total[...] = jnp.zeros(total.shape, F32)
    acc[...] = jnp.zeros(acc.shape, F32)
    forward_pairs(
        count, q_ref, k_ref, v_ref, tile_of, place_of, (s0, m0), (s1, m1), top, total, acc
    )


def forward_halo_kernel(
    pattern_ref, q_ref, top_in, total_in, acc_in, above_ref, below_ref, early_ref,
    att_ref, flip_ref, lse_ref,
    kband, vband, tile_of, place_of, s0, s1, m0, m1, top, total, acc, sem,
):
    copies = fill_band((above_ref, below_ref), kband, vband, sem)
    count = build_pairs(pattern_ref, tile_of, place_of, (0, 2))
    top[...] = top_in[...]
    total[...] = total_in[...]
    acc[...] = acc_in[...]
    for copy in copies:
        copy.wait()
    forward_pairs(
        count, q_ref, kband, vband, tile_of, place_of, (s0, m0), (s1, m1), top, total, acc
    )
    for tile in range(ROW_TILES):
        attended = acc[tile] / total[tile]
        flip_ref[tile] = attended.astype(BF)
        att_ref[tile] = attended.T.astype(BF)
        lse_ref[tile] = top[tile] + jnp.log2(total[tile])


def backward_pairs(
    count, q_ref, back, att_ref, lse_ref, kband, vband, tile_of, place_of,
    even, odd, delta, dk, dv, dq,
):
    for tile in range(ROW_TILES):
        prod = back[tile].astype(F32) * att_ref[tile].astype(F32)
        delta[tile] = jnp.sum(prod, axis=0, keepdims=True)

    def make(slot, i):
        tile, place = tile_of[i], place_of[i]
        scores = dot(kband[place], q_ref[tile], NT) * (SCALING * LOG2E)
        prob = jnp.exp2(scores - lse_ref[tile])
        prob_grad = dot(vband[place], back[tile], NN)
        slot[0][...] = prob.astype(BF)
        slot[1][...] = (prob * (prob_grad - delta[tile])).astype(BF)

    def use(slot, i):
        tile, place = tile_of[i], place_of[i]
        dv[place] += dot(slot[0][...], back[tile], NT)
        dk[place] += dot(slot[1][...], q_ref[tile], NN)
        dq[tile] += dot(kband[place], slot[1][...], TN)

    run_pairs(count, make, use, even, odd)


def backward_halo_kernel(
    pattern_ref, q_ref, back_mine_ref, back_got_ref, att_ref, lse_ref, above_ref, below_ref,
    up_ref, down_ref, dq, back_ref, zero_ref,
    kband, vband, tile_of, place_of, p0, p1, d0, d1, delta, dk, dv, sem,
):
    copies = fill_band((above_ref, below_ref), kband, vband, sem)
    count = build_pairs(pattern_ref, tile_of, place_of, (0, 2))
    dk[...] = jnp.zeros(dk.shape, F32)
    dv[...] = jnp.zeros(dv.shape, F32)
    dq[...] = jnp.zeros(dq.shape, F32)
    zero_ref[...] = jnp.zeros(zero_ref.shape, F32)
    for tile in range(ROW_TILES):
        cols = pl.ds(tile * TILE, TILE)
        back_ref[tile] = (back_mine_ref[:, cols] + back_got_ref[:, cols].astype(F32)).astype(BF)
    for copy in copies:
        copy.wait()
    backward_pairs(
        count, q_ref, back_ref, att_ref, lse_ref, kband, vband, tile_of, place_of,
        (p0, d0), (p1, d1), delta, dk, dv, dq,
    )
    for i in range(ROW_TILES):
        up_ref[0, i] = dk[i].astype(BF)
        up_ref[1, i] = dv[i].astype(BF)
        down_ref[0, i] = dk[ROW_TILES + i].astype(BF)
        down_ref[1, i] = dv[ROW_TILES + i].astype(BF)


def backward_own_kernel(
    pattern_ref, q_ref, back_ref, att_ref, lse_ref, k_ref, v_ref, dq_in, up_ref, down_ref,
    dq_ref, dk_ref, dv_ref,
    tile_of, place_of, p0, p1, d0, d1, delta, dq, dk, dv,
):
    count = build_pairs(pattern_ref, tile_of, place_of, (1,))
    dk[...] = up_ref[0].astype(F32) + down_ref[0].astype(F32)
    dv[...] = up_ref[1].astype(F32) + down_ref[1].astype(F32)
    dq[...] = dq_in[...]
    backward_pairs(
        count, q_ref, back_ref, att_ref, lse_ref, k_ref, v_ref, tile_of, place_of,
        (p0, d0), (p1, d1), delta, dk, dv, dq,
    )
    for tile in range(ROW_TILES):
        dq_ref[tile] = (dq[tile] * SCALING).T.astype(BF)
        dk_ref[tile] = (dk[tile] * SCALING).astype(BF)
        dv_ref[tile] = dv[tile].astype(BF)


def back_kernel(place_ref, other_ref, mine_ref, *refs):
    blocks, (grad, sent_ref, kept_ref) = refs[:-3], refs[-3:]
    rows, tokens = blocks[0].shape

    def at(offset):
        source = lax.rem(place_ref[2] + offset + 8, 8)
        return pl.ds(pl.multiple_of(source * rows, 32), rows)

    for offset, block in zip(RING, blocks):
        grad[at(offset)] = block[...]
    grad[at(4), : tokens // 2] = blocks[-2][...]
    grad[at(4), tokens // 2 :] = blocks[-1][...]
    sent_ref[...] = dot(other_ref[...], grad[...], NN).astype(BF)
    kept_ref[...] = dot(mine_ref[...], grad[...], NN)


def part_kernel(place_ref, mine_ref, other_ref, att_ref, got_ref, early_ref, *refs):
    blocks, (weights, heads, total) = refs[:-3], refs[-3:]
    rows, tokens = blocks[0].shape
    weights[:HDIM] = mine_ref[...]
    weights[HDIM:] = other_ref[...]
    heads[:, :HDIM] = att_ref[...]
    heads[:, HDIM:] = got_ref[...]
    for tile in range(ROW_TILES):
        cols = slice(tile * TILE, (tile + 1) * TILE)
        terms = dot(weights[...], heads[cols], (((0,), (1,)), ((), ())))
        total[:, cols] = terms.astype(BF)

    def at(offset):
        target = lax.rem(place_ref[2] + offset + 8, 8)
        return pl.ds(pl.multiple_of(target * rows, 32), rows)

    for offset, block in zip(RING, blocks):
        block[...] = total[at(offset)]
    blocks[-2][...] = total[at(4), : tokens // 2]
    blocks[-1][...] = total[at(4), tokens // 2 :]


def arrived_kernel(up_ref, down_ref, zero_ref):
    zero_ref[...] = jnp.zeros(zero_ref.shape, F32)


def weight_kernel(place_ref, grad_ref, att_ref, other_ref, early_ref, send_ref, keep_ref, heads, total):
    half, core = place_ref[0], place_ref[1]
    heads[:, pl.ds(pl.multiple_of(half * HDIM, HDIM), HDIM)] = att_ref[...]
    heads[:, pl.ds(pl.multiple_of((1 - half) * HDIM, HDIM), HDIM)] = other_ref[...]
    total[...] = dot(grad_ref[...], heads[...], NN)
    rows = send_ref.shape[3]
    for low in range(2):
        for xh in range(2):
            chunk = low * 4 + xh * 2
            mine = pl.ds(pl.multiple_of((chunk + core) * rows, 8), rows)
            yours = pl.ds(pl.multiple_of((chunk + 1 - core) * rows, 8), rows)
            for a in range(2):
                lanes = slice(a * HDIM, (a + 1) * HDIM)
                keep_ref[a, low, xh] = total[mine, lanes]
                send_ref[a, low, xh] = total[yours, lanes].astype(BF)


VM = pl.BlockSpec(memory_space=pltpu.VMEM)
SM = pl.BlockSpec(memory_space=pltpu.SMEM)
HB = pl.BlockSpec(memory_space=pltpu.HBM)
ANY = pl.BlockSpec(memory_space=pl.ANY)
BLOCK = (ROW_TILES, TILE, HDIM)
FLIP = (ROW_TILES, HDIM, TILE)
LINE = (ROW_TILES, 1, TILE)
RING = (0, -1, 1, -2, 2, -3, 3)
HALO = (2 * ROW_TILES, TILE, HDIM)
PAIR_LISTS = [pltpu.SMEM((49,), jnp.int32), pltpu.SMEM((49,), jnp.int32)]
HALO_BAND = [pltpu.VMEM(HALO, BF), pltpu.VMEM(HALO, BF)]
SCORES = [pltpu.VMEM((TILE, TILE), F32)] * 2 + [pltpu.VMEM((1, TILE), F32)] * 2
TERMS = [pltpu.VMEM((TILE, TILE), BF)] * 4
DMA_SEMS = pltpu.SemaphoreType.DMA((4,))


def kernel_call(kernel, name, outs, in_specs, scratch, flops):
    return pl.pallas_call(
        kernel,
        name=name,
        out_shape=tuple(jax.ShapeDtypeStruct(shape, kind) for shape, kind in outs),
        in_specs=in_specs,
        out_specs=(VM,) * len(outs),
        scratch_shapes=scratch,
        compiler_params=pltpu.CompilerParams(vmem_limit_bytes=32 * 1024 * 1024),
        cost_estimate=pl.CostEstimate(
            flops=flops, bytes_accessed=4_000_000, transcendentals=3_000_000
        ),
    )


def forward_own(*args):
    return kernel_call(
        forward_own_kernel, "forward_own", [(LINE, F32), (LINE, F32), (FLIP, F32)],
        [SM, VM, VM, VM, ANY, ANY], PAIR_LISTS + SCORES, 3_000_000_000,
    )(*args)


def forward_halo(*args):
    state = [pltpu.VMEM(LINE, F32), pltpu.VMEM(LINE, F32), pltpu.VMEM(FLIP, F32)]
    return kernel_call(
        forward_halo_kernel, "forward_halo", [(BLOCK, BF), (FLIP, BF), (LINE, F32)],
        [SM] + [VM] * 4 + [HB] * 2 + [ANY], HALO_BAND + PAIR_LISTS + SCORES + state + [DMA_SEMS],
        5_000_000_000,
    )(*args)


def backward_halo(*args):
    outs = [((2,) + BLOCK, BF), ((2,) + BLOCK, BF), (FLIP, F32), (FLIP, BF), ((1, HDIM), F32)]
    return kernel_call(
        backward_halo_kernel, "backward_halo", outs, [SM] + [VM] * 5 + [HB] * 2,
        HALO_BAND + PAIR_LISTS + TERMS
        + [pltpu.VMEM(LINE, F32), pltpu.VMEM(HALO, F32), pltpu.VMEM(HALO, F32), DMA_SEMS],
        12_000_000_000,
    )(*args)


def backward_own(*args):
    outs = [(BLOCK, BF), (BLOCK, BF), (BLOCK, BF)]
    return kernel_call(
        backward_own_kernel, "backward_own", outs, [SM] + [VM] * 9,
        PAIR_LISTS + TERMS
        + [pltpu.VMEM(LINE, F32), pltpu.VMEM(FLIP, F32)] + [pltpu.VMEM(BLOCK, F32)] * 2,
        6_000_000_000,
    )(*args)


def back_parts(place, w_other, w_mine, blocks):
    heads, feats = w_mine.shape
    tokens = blocks[0].shape[1]
    outs = [((feats, tokens), BF), ((heads, tokens), BF), ((heads, tokens), F32)]
    return kernel_call(
        back_kernel, "back_parts", outs, [SM] + [VM] * (2 + len(blocks)), [], 2_000_000_000
    )(place, w_other, w_mine, *blocks)


def projected_parts(place, w_mine, *args):
    feats, tokens = w_mine.shape[1], ROW_TILES * TILE
    outs = [((feats // 8, tokens), BF)] * 7 + [((feats // 8, tokens // 2), BF)] * 2
    return kernel_call(
        part_kernel, "projected_parts", outs, [SM] + [VM] * 4 + [ANY],
        [
            pltpu.VMEM((2 * HDIM, feats), BF),
            pltpu.VMEM((tokens, 2 * HDIM), BF),
            pltpu.VMEM((feats, tokens), BF),
        ],
        2_000_000_000,
    )(place, w_mine, *args)


def arrived(up, down):
    return kernel_call(arrived_kernel, "arrived", [((1, HDIM), F32)], [ANY] * 2, [], 1000)(up, down)[0]


def weight_parts(place, grad_half, att, att_other, early):
    feats, tokens = grad_half.shape
    shape = (2, 2, 2, feats // 8, HDIM)
    return kernel_call(
        weight_kernel, "weight_parts", [(shape, BF), (shape, F32)], [SM] + [VM] * 3 + [ANY],
        [pltpu.VMEM((tokens, 2 * HDIM), BF), pltpu.VMEM((feats, 2 * HDIM), F32)],
        2_000_000_000,
    )(place, grad_half, att, att_other, early)


def shifted(block, distance):
    route = [(i - distance, i) for i in range(16) if 0 <= i - distance < 16]
    return lax.ppermute(block, ST, route)


def swapped(block):
    return lax.ppermute(block, "xl", [(0, 1), (1, 0)])


def halved(part, axis, distance, size, dim, bit):
    route = [(i, i ^ distance) for i in range(size)]
    send = lax.dynamic_index_in_dim(part, 1 - bit, dim, keepdims=False).astype(BF)
    keep = lax.dynamic_index_in_dim(part, bit, dim, keepdims=False)
    return keep, lax.ppermute(send, axis, route)


def ring_gathered(block):
    size = lax.axis_size("z")
    onward = [(i, (i + 1) % size) for i in range(size)]
    backward = [(j, i) for i, j in onward]
    right = left = block
    got = [block]
    for _ in range(size // 2 - 1):
        right, left = lax.ppermute(right, "z", onward), lax.ppermute(left, "z", backward)
        got += [right, left]
    middle = block.shape[1] // 2
    far = [lax.ppermute(right[:, :middle], "z", onward), lax.ppermute(left[:, middle:], "z", backward)]
    return got + far


def ring_summed(parts, late):
    size = lax.axis_size("z")
    onward = [(i, (i + 1) % size) for i in range(size)]
    backward = [(j, i) for i, j in onward]
    middle = parts[-1].shape[1]
    first = lax.ppermute(parts[-2], "z", onward)
    right = first.astype(F32)
    left = lax.ppermute(parts[-1], "z", backward).astype(F32)
    by_offset = {offset: part.astype(F32) for offset, part in zip(RING, parts)}
    last = size // 2 - 1
    right = jnp.concatenate((by_offset[last][:, :middle] + right, by_offset[last][:, middle:]), axis=1)
    left = jnp.concatenate((by_offset[-last][:, :middle], by_offset[-last][:, middle:] + left), axis=1)
    for offset in range(last - 1, -1, -1):
        if offset == 0:
            right, left = right + late, left + late
        right = lax.ppermute(right.astype(BF), "z", onward).astype(F32)
        left = lax.ppermute(left.astype(BF), "z", backward).astype(F32)
        if offset:
            right, left = right + by_offset[offset], left + by_offset[-offset]
    return right + left + by_offset[0], first


def body(queries, key_rows, value_rows, out_grad, proj_weight, pattern):
    half, y = lax.axis_index("xl"), lax.axis_index("y")
    tokens = queries.shape[1]
    place = jnp.stack((half, lax.axis_index("core"), lax.axis_index("z"))).astype(jnp.int32)
    places = lax.axis_size("z")
    q = queries.reshape(BLOCK)
    keys, values = key_rows.reshape(BLOCK), value_rows.reshape(BLOCK)
    kv = jnp.stack((keys, values))
    above, below = shifted(kv, 1), shifted(kv, -1)

    block = out_grad[0].T
    feats = places * block.shape[0]
    blocks = ring_gathered(block)
    w_mine = lax.dynamic_slice_in_dim(proj_weight, half * feats, feats, 1)
    w_other = swapped(lax.dynamic_slice_in_dim(proj_weight, (1 - half) * feats, feats, 1))

    grad_half, back_sent, back_mine = back_parts(place, w_other, w_mine, blocks)
    back_got = swapped(back_sent)

    own_state = forward_own(pattern, q, keys, values, above, below)
    attended, att_flip, lse = forward_halo(pattern, q, *own_state, above, below, back_sent)
    att = attended.reshape(tokens, HDIM)
    att_other = swapped(att)

    up, down, dq_part, back, zero = backward_halo(
        pattern, q, back_mine, back_got, att_flip, lse, above, below
    )
    up, down = shifted(up, -1), shifted(down, 1)
    late = arrived(up, down)
    dq, dk, dv = backward_own(
        pattern, q, back, att_flip, lse, keys, values, dq_part, up, down
    )

    parts = projected_parts(place, w_mine, w_other, att, att_other, zero)
    projected, first = ring_summed(parts, late[:, :1])
    projected = projected.astype(BF).T[None]

    sent, kept = weight_parts(place, grad_half, att, att_other, first)
    got = lax.ppermute(sent, "core", [(0, 1), (1, 0)])
    kept, got = halved(kept + got.astype(F32), "xh", 1, 2, 2, lax.axis_index("xh"))

    kept = (kept + got.astype(F32)).astype(BF).reshape((4,) + kept.shape[2:])
    summed = 0.0
    for k in range(4):
        piece = lax.dynamic_index_in_dim(kept, y ^ k, 0, keepdims=False)
        route = [
            (h * 4 + i, (i ^ k) // 2 * 4 + 2 * h + (i ^ k) % 2) for h in range(2) for i in range(4)
        ]
        summed = summed + lax.ppermute(piece, ("xl", "y"), route).astype(F32)
    weight_grad = summed.T

    shape = (1, tokens, HDIM)
    return projected, dq.reshape(shape), dk.reshape(shape), dv.reshape(shape), weight_grad


def solution(mesh):
    fine = Mesh(mesh.devices.reshape(2, 8, 4, 2, 2), ("xl", "z", "y", "xh", "core"))
    fsdp = ("xl", "z")
    rows = P(None, ST, fsdp)
    return jax.shard_map(
        body,
        mesh=fine,
        in_specs=(rows, rows, rows, rows, P(fsdp, None), P(ST, None)),
        out_specs=(rows, rows, rows, rows, P(fsdp, ST)),
        check_vma=False,
    )
```

```python
import functools

import jax
import jax.numpy as jnp
from jax import lax
from jax.experimental import pallas as pl
from jax.experimental.pallas import tpu as pltpu
from jax.sharding import Mesh
from jax.sharding import PartitionSpec as P

HDIM = 128
TILE = 384
TF = 2
TC = 2
ROW_TILES = TF * TC
BAND = 3 * ROW_TILES
SCALING = HDIM ** (-0.5)
LOG2E = 1.4426950408889634
BF = jnp.bfloat16
F32 = jnp.float32
ST = ("y", "xh", "core")
NT = (((1,), (1,)), ((), ()))
TN = (((0,), (0,)), ((), ()))
NN = (((1,), (0,)), ((), ()))


def dot(a, b, dims):
    return lax.dot_general(a, b, dims, preferred_element_type=F32)


def build_pairs(pattern_ref, tile_of, place_of, rows):
    count = jnp.int32(0)
    for tile in range(ROW_TILES):
        frame, col = tile // TC, tile % TC
        for at, row in enumerate(rows):
            for inner in range(ROW_TILES):
                slot = (inner // TC - frame + 1) * 9 + row * 3 + (inner % TC - col + 1)
                tile_of[count] = jnp.int32(tile)
                place_of[count] = jnp.int32(at * ROW_TILES + inner)
                count = count + (pattern_ref[tile, slot] >= 0).astype(jnp.int32)
    return count


def run_pairs(count, make, use, even, odd):
    make(even, 0)

    def step(j, carry):
        i = 2 * j
        make(odd, i + 1)
        use(even, i)
        make(even, i + 2)
        use(odd, i + 1)
        return carry

    lax.fori_loop(0, (count - 1) // 2, step, 0)

    @pl.when(count % 2 == 1)
    def _():
        use(even, count - 1)

    @pl.when(count % 2 == 0)
    def _():
        make(odd, count - 1)
        use(even, count - 2)
        use(odd, count - 1)


def fill_band(refs, kband, vband, sem):
    copies = []
    for i, ref in enumerate(refs):
        place = pl.ds(i * ROW_TILES, ROW_TILES)
        copies.append(pltpu.make_async_copy(ref.at[0], kband.at[place], sem.at[2 * i]))
        copies.append(pltpu.make_async_copy(ref.at[1], vband.at[place], sem.at[2 * i + 1]))
    for copy in copies:
        copy.start()
    return copies


def forward_pairs(count, q_ref, kband, vband, tile_of, place_of, even, odd, top, total, acc):
    def make(slot, i):
        scores = dot(kband[place_of[i]], q_ref[tile_of[i]], NT) * (SCALING * LOG2E)
        slot[0][...] = scores
        slot[1][...] = jnp.max(scores, axis=0, keepdims=True)

    def use(slot, i):
        tile = tile_of[i]
        before = top[tile]
        peak = jnp.maximum(before, slot[1][...])
        shrink = jnp.exp2(before - peak)
        raised = jnp.exp2(slot[0][...] - peak)
        top[tile] = peak
        total[tile] = shrink * total[tile] + jnp.sum(raised, axis=0, keepdims=True)
        acc[tile] = shrink * acc[tile] + dot(vband[place_of[i]], raised.astype(BF), TN)

    run_pairs(count, make, use, even, odd)


def forward_own_kernel(
    pattern_ref, q_ref, k_ref, v_ref, top, total, acc, tile_of, place_of, s0, s1, m0, m1
):
    count = build_pairs(pattern_ref, tile_of, place_of, (1,))
    top[...] = jnp.full(top.shape, -jnp.inf, F32)
    total[...] = jnp.zeros(total.shape, F32)
    acc[...] = jnp.zeros(acc.shape, F32)
    forward_pairs(
        count, q_ref, k_ref, v_ref, tile_of, place_of, (s0, m0), (s1, m1), top, total, acc
    )


def forward_halo_kernel(
    pattern_ref, q_ref, top_in, total_in, acc_in, above_ref, below_ref, early_ref,
    att_ref, flip_ref, lse_ref,
    kband, vband, tile_of, place_of, s0, s1, m0, m1, top, total, acc, sem,
):
    copies = fill_band((above_ref, below_ref), kband, vband, sem)
    count = build_pairs(pattern_ref, tile_of, place_of, (0, 2))
    top[...] = top_in[...]
    total[...] = total_in[...]
    acc[...] = acc_in[...]
    for copy in copies:
        copy.wait()
    forward_pairs(
        count, q_ref, kband, vband, tile_of, place_of, (s0, m0), (s1, m1), top, total, acc
    )
    for tile in range(ROW_TILES):
        attended = acc[tile] / total[tile]
        flip_ref[tile] = attended.astype(BF)
        att_ref[tile] = attended.T.astype(BF)
        lse_ref[tile] = top[tile] + jnp.log2(total[tile])


def backward_pairs(
    count, q_ref, back, att_ref, lse_ref, kband, vband, tile_of, place_of,
    even, odd, delta, dk, dv, dq,
):
    for tile in range(ROW_TILES):
        prod = back[tile].astype(F32) * att_ref[tile].astype(F32)
        delta[tile] = jnp.sum(prod, axis=0, keepdims=True)

    def make(slot, i):
        tile, place = tile_of[i], place_of[i]
        scores = dot(kband[place], q_ref[tile], NT) * (SCALING * LOG2E)
        prob = jnp.exp2(scores - lse_ref[tile])
        prob_grad = dot(vband[place], back[tile], NN)
        slot[0][...] = prob.astype(BF)
        slot[1][...] = (prob * (prob_grad - delta[tile])).astype(BF)

    def use(slot, i):
        tile, place = tile_of[i], place_of[i]
        dv[place] += dot(slot[0][...], back[tile], NT)
        dk[place] += dot(slot[1][...], q_ref[tile], NN)
        dq[tile] += dot(kband[place], slot[1][...], TN)

    run_pairs(count, make, use, even, odd)


def backward_halo_kernel(
    pattern_ref, q_ref, back_mine_ref, back_got_ref, att_ref, lse_ref, above_ref, below_ref,
    early_ref,
    up_ref, down_ref, dq, back_ref, zero_ref,
    kband, vband, tile_of, place_of, p0, p1, d0, d1, delta, dk, dv, sem,
):
    copies = fill_band((above_ref, below_ref), kband, vband, sem)
    count = build_pairs(pattern_ref, tile_of, place_of, (0, 2))
    dk[...] = jnp.zeros(dk.shape, F32)
    dv[...] = jnp.zeros(dv.shape, F32)
    dq[...] = jnp.zeros(dq.shape, F32)
    zero_ref[...] = jnp.zeros(zero_ref.shape, F32)
    for tile in range(ROW_TILES):
        cols = pl.ds(tile * TILE, TILE)
        back_ref[tile] = (back_mine_ref[:, cols] + back_got_ref[:, cols].astype(F32)).astype(BF)
    for copy in copies:
        copy.wait()
    backward_pairs(
        count, q_ref, back_ref, att_ref, lse_ref, kband, vband, tile_of, place_of,
        (p0, d0), (p1, d1), delta, dk, dv, dq,
    )
    for i in range(ROW_TILES):
        up_ref[0, i] = dk[i].astype(BF)
        up_ref[1, i] = dv[i].astype(BF)
        down_ref[0, i] = dk[ROW_TILES + i].astype(BF)
        down_ref[1, i] = dv[ROW_TILES + i].astype(BF)


def backward_own_kernel(
    pattern_ref, q_ref, back_ref, att_ref, lse_ref, k_ref, v_ref, dq_in, early_ref,
    dq_ref, dk, dv, zero_ref,
    tile_of, place_of, p0, p1, d0, d1, delta, dq,
):
    count = build_pairs(pattern_ref, tile_of, place_of, (1,))
    dk[...] = jnp.zeros(dk.shape, F32)
    dv[...] = jnp.zeros(dv.shape, F32)
    zero_ref[...] = jnp.zeros(zero_ref.shape, F32)
    dq[...] = dq_in[...]
    backward_pairs(
        count, q_ref, back_ref, att_ref, lse_ref, k_ref, v_ref, tile_of, place_of,
        (p0, d0), (p1, d1), delta, dk, dv, dq,
    )
    for tile in range(ROW_TILES):
        dq_ref[tile] = (dq[tile] * SCALING).T.astype(BF)


def made_kernel(array_ref, zero_ref):
    zero_ref[...] = jnp.zeros(zero_ref.shape, F32)


def weight_kernel(place_ref, grad_ref, att_ref, other_ref, early_ref, send_ref, keep_ref, heads, total):
    half, core = place_ref[0], place_ref[1]
    heads[:, pl.ds(pl.multiple_of(half * HDIM, HDIM), HDIM)] = att_ref[...]
    heads[:, pl.ds(pl.multiple_of((1 - half) * HDIM, HDIM), HDIM)] = other_ref[...]
    total[...] = dot(grad_ref[...], heads[...], NN)
    rows = send_ref.shape[3]
    for low in range(2):
        for xh in range(2):
            chunk = low * 4 + xh * 2
            mine = pl.ds(pl.multiple_of((chunk + core) * rows, 8), rows)
            yours = pl.ds(pl.multiple_of((chunk + 1 - core) * rows, 8), rows)
            for a in range(2):
                lanes = slice(a * HDIM, (a + 1) * HDIM)
                keep_ref[a, low, xh] = total[mine, lanes]
                send_ref[a, low, xh] = total[yours, lanes].astype(BF)


VM = pl.BlockSpec(memory_space=pltpu.VMEM)
SM = pl.BlockSpec(memory_space=pltpu.SMEM)
HB = pl.BlockSpec(memory_space=pltpu.HBM)
BLOCK = (ROW_TILES, TILE, HDIM)
FLIP = (ROW_TILES, HDIM, TILE)
LINE = (ROW_TILES, 1, TILE)
HALO = (2 * ROW_TILES, TILE, HDIM)
PAIR_LISTS = [pltpu.SMEM((49,), jnp.int32), pltpu.SMEM((49,), jnp.int32)]
HALO_BAND = [pltpu.VMEM(HALO, BF), pltpu.VMEM(HALO, BF)]
SCORES = [pltpu.VMEM((TILE, TILE), F32)] * 2 + [pltpu.VMEM((1, TILE), F32)] * 2
TERMS = [pltpu.VMEM((TILE, TILE), BF)] * 4
DMA_SEMS = pltpu.SemaphoreType.DMA((4,))


def kernel_call(kernel, name, outs, in_specs, scratch, flops):
    return pl.pallas_call(
        kernel,
        name=name,
        out_shape=tuple(jax.ShapeDtypeStruct(shape, kind) for shape, kind in outs),
        in_specs=in_specs,
        out_specs=(VM,) * len(outs),
        scratch_shapes=scratch,
        compiler_params=pltpu.CompilerParams(vmem_limit_bytes=32 * 1024 * 1024),
        cost_estimate=pl.CostEstimate(
            flops=flops, bytes_accessed=4_000_000, transcendentals=3_000_000
        ),
    )


def forward_own(*args):
    return kernel_call(
        forward_own_kernel, "forward_own", [(LINE, F32), (LINE, F32), (FLIP, F32)],
        [SM, VM, VM, VM], PAIR_LISTS + SCORES, 3_000_000_000,
    )(*args)


def forward_halo(*args):
    state = [pltpu.VMEM(LINE, F32), pltpu.VMEM(LINE, F32), pltpu.VMEM(FLIP, F32)]
    return kernel_call(
        forward_halo_kernel, "forward_halo", [(BLOCK, BF), (FLIP, BF), (LINE, F32)],
        [SM] + [VM] * 4 + [HB] * 3, HALO_BAND + PAIR_LISTS + SCORES + state + [DMA_SEMS],
        5_000_000_000,
    )(*args)


def backward_halo(*args):
    outs = [((2,) + BLOCK, BF), ((2,) + BLOCK, BF), (FLIP, F32), (FLIP, BF), ((1, HDIM), F32)]
    return kernel_call(
        backward_halo_kernel, "backward_halo", outs, [SM] + [VM] * 5 + [HB] * 3,
        HALO_BAND + PAIR_LISTS + TERMS
        + [pltpu.VMEM(LINE, F32), pltpu.VMEM(HALO, F32), pltpu.VMEM(HALO, F32), DMA_SEMS],
        12_000_000_000,
    )(*args)


def backward_own(*args):
    outs = [(BLOCK, BF), (BLOCK, F32), (BLOCK, F32), ((1, HDIM), F32)]
    return kernel_call(
        backward_own_kernel, "backward_own", outs, [SM] + [VM] * 7 + [HB],
        PAIR_LISTS + TERMS + [pltpu.VMEM(LINE, F32), pltpu.VMEM(FLIP, F32)],
        6_000_000_000,
    )(*args)


def made(array):
    any_space = pl.BlockSpec(memory_space=pl.ANY)
    return kernel_call(made_kernel, "made", [((1, HDIM), F32)], [any_space], [], 1000)(array)[0]


def weight_parts(place, grad_half, att, att_other, early):
    feats, tokens = grad_half.shape
    shape = (2, 2, 2, feats // 8, HDIM)
    return kernel_call(
        weight_kernel, "weight_parts", [(shape, BF), (shape, F32)], [SM] + [VM] * 3 + [HB],
        [pltpu.VMEM((tokens, 2 * HDIM), BF), pltpu.VMEM((feats, 2 * HDIM), F32)],
        2_000_000_000,
    )(place, grad_half, att, att_other, early)


def shifted(block, distance):
    route = [(i - distance, i) for i in range(16) if 0 <= i - distance < 16]
    return lax.ppermute(block, ST, route)


def swapped(block):
    return lax.ppermute(block, "xl", [(0, 1), (1, 0)])


def halved(part, axis, distance, size, dim, bit):
    route = [(i, i ^ distance) for i in range(size)]
    send = lax.dynamic_index_in_dim(part, 1 - bit, dim, keepdims=False).astype(BF)
    keep = lax.dynamic_index_in_dim(part, bit, dim, keepdims=False)
    return keep, lax.ppermute(send, axis, route)


def body(queries, key_rows, value_rows, out_grad, proj_weight, pattern):
    half, y = lax.axis_index("xl"), lax.axis_index("y")
    tokens = queries.shape[1]
    place = jnp.stack((half, lax.axis_index("core"))).astype(jnp.int32)
    q = queries.reshape(BLOCK)
    keys, values = key_rows.reshape(BLOCK), value_rows.reshape(BLOCK)
    kv = jnp.stack((keys, values))
    above, below = shifted(kv, 1), shifted(kv, -1)

    grad_half = lax.all_gather(out_grad[0].T, "z", axis=0, tiled=True)
    feats = grad_half.shape[0]
    w_mine = lax.dynamic_slice_in_dim(proj_weight, half * feats, feats, 1)
    w_other = swapped(lax.dynamic_slice_in_dim(proj_weight, (1 - half) * feats, feats, 1))

    own_state = forward_own(pattern, q, keys, values)
    attended, att_flip, lse = forward_halo(pattern, q, *own_state, above, below, w_other)
    att = attended.reshape(tokens, HDIM)
    att_other = swapped(att)

    back_sent = dot(w_other, grad_half, NN).astype(BF)
    back_got = swapped(back_sent)
    back_mine = dot(w_mine, grad_half, NN)

    by_rows = (((0,), (1,)), ((), ()))
    part = dot(w_mine, att, by_rows) + dot(w_other, att_other, by_rows)
    part = part + made(back_sent)[:, :1]
    projected = lax.psum_scatter(part.astype(BF), "z", scatter_dimension=0, tiled=True)
    projected = projected.T[None]

    sent, kept = weight_parts(place, grad_half, att, att_other, back_sent)
    got = lax.ppermute(sent, "core", [(0, 1), (1, 0)])
    kept, got = halved(kept + got.astype(F32), "xh", 1, 2, 2, lax.axis_index("xh"))

    up, down, dq_part, back, _ = backward_halo(
        pattern, q, back_mine, back_got, att_flip, lse, above, below, sent
    )
    up, down = shifted(up, -1), shifted(down, 1)
    dq, dk, dv, zero = backward_own(pattern, q, back, att_flip, lse, keys, values, dq_part, kept)

    kept = (kept + got.astype(F32) + zero).astype(BF).reshape((4,) + kept.shape[2:])
    summed = 0.0
    for k in range(4):
        piece = lax.dynamic_index_in_dim(kept, y ^ k, 0, keepdims=False)
        route = [
            (h * 4 + i, (i ^ k) // 2 * 4 + 2 * h + (i ^ k) % 2) for h in range(2) for i in range(4)
        ]
        summed = summed + lax.ppermute(piece, ("xl", "y"), route).astype(F32)
    weight_grad = summed.T

    shape = (1, tokens, HDIM)
    key_grad = SCALING * (dk + up[0].astype(F32) + down[0].astype(F32))
    value_grad = dv + up[1].astype(F32) + down[1].astype(F32)
    key_grad = key_grad.astype(BF).reshape(shape)
    value_grad = value_grad.astype(BF).reshape(shape)
    return projected, dq.reshape(shape), key_grad, value_grad, weight_grad


def solution(mesh):
    fine = Mesh(mesh.devices.reshape(2, 8, 4, 2, 2), ("xl", "z", "y", "xh", "core"))
    fsdp = ("xl", "z")
    rows = P(None, ST, fsdp)
    return jax.shard_map(
        body,
        mesh=fine,
        in_specs=(rows, rows, rows, rows, P(fsdp, None), P(ST, None)),
        out_specs=(rows, rows, rows, rows, P(fsdp, ST)),
        check_vma=False,
    )
```

```python
import functools

import jax
import jax.numpy as jnp
from jax import lax
from jax.experimental import pallas as pl
from jax.experimental.pallas import tpu as pltpu
from jax.sharding import Mesh
from jax.sharding import PartitionSpec as P

HDIM = 128
TILE = 384
TF = 2
TC = 2
ROW_TILES = TF * TC
BAND = 3 * ROW_TILES
SCALING = HDIM ** (-0.5)
LOG2E = 1.4426950408889634
BF = jnp.bfloat16
F32 = jnp.float32
ST = ("y", "xh", "core")
NT = (((1,), (1,)), ((), ()))
TN = (((0,), (0,)), ((), ()))
NN = (((1,), (0,)), ((), ()))


def dot(a, b, dims):
    return lax.dot_general(a, b, dims, preferred_element_type=F32)


def build_pairs(pattern_ref, tile_of, place_of, rows):
    count = jnp.int32(0)
    for tile in range(ROW_TILES):
        frame, col = tile // TC, tile % TC
        for at, row in enumerate(rows):
            for inner in range(ROW_TILES):
                slot = (inner // TC - frame + 1) * 9 + row * 3 + (inner % TC - col + 1)
                tile_of[count] = jnp.int32(tile)
                place_of[count] = jnp.int32(at * ROW_TILES + inner)
                count = count + (pattern_ref[tile, slot] >= 0).astype(jnp.int32)
    return count


def run_pairs(count, make, use, even, odd):
    make(even, 0)

    def step(j, carry):
        i = 2 * j
        make(odd, i + 1)
        use(even, i)
        make(even, i + 2)
        use(odd, i + 1)
        return carry

    lax.fori_loop(0, (count - 1) // 2, step, 0)

    @pl.when(count % 2 == 1)
    def _():
        use(even, count - 1)

    @pl.when(count % 2 == 0)
    def _():
        make(odd, count - 1)
        use(even, count - 2)
        use(odd, count - 1)


def fill_band(refs, kband, vband, sem):
    copies = []
    for i, ref in enumerate(refs):
        place = pl.ds(i * ROW_TILES, ROW_TILES)
        copies.append(pltpu.make_async_copy(ref.at[0], kband.at[place], sem.at[2 * i]))
        copies.append(pltpu.make_async_copy(ref.at[1], vband.at[place], sem.at[2 * i + 1]))
    for copy in copies:
        copy.start()
    return copies


def forward_pairs(count, q_ref, kband, vband, tile_of, place_of, even, odd, top, total, acc):
    def make(slot, i):
        scores = dot(kband[place_of[i]], q_ref[tile_of[i]], NT) * (SCALING * LOG2E)
        slot[0][...] = scores
        slot[1][...] = jnp.max(scores, axis=0, keepdims=True)

    def use(slot, i):
        tile = tile_of[i]
        before = top[tile]
        peak = jnp.maximum(before, slot[1][...])
        shrink = jnp.exp2(before - peak)
        raised = jnp.exp2(slot[0][...] - peak)
        top[tile] = peak
        total[tile] = shrink * total[tile] + jnp.sum(raised, axis=0, keepdims=True)
        acc[tile] = shrink * acc[tile] + dot(vband[place_of[i]], raised.astype(BF), TN)

    run_pairs(count, make, use, even, odd)


def forward_own_kernel(
    pattern_ref, q_ref, k_ref, v_ref, top, total, acc, tile_of, place_of, s0, s1, m0, m1
):
    count = build_pairs(pattern_ref, tile_of, place_of, (1,))
    top[...] = jnp.full(top.shape, -jnp.inf, F32)
    total[...] = jnp.zeros(total.shape, F32)
    acc[...] = jnp.zeros(acc.shape, F32)
    forward_pairs(
        count, q_ref, k_ref, v_ref, tile_of, place_of, (s0, m0), (s1, m1), top, total, acc
    )


def forward_halo_kernel(
    pattern_ref, q_ref, top_in, total_in, acc_in, above_ref, below_ref, early_ref,
    att_ref, flip_ref, lse_ref,
    kband, vband, tile_of, place_of, s0, s1, m0, m1, top, total, acc, sem,
):
    copies = fill_band((above_ref, below_ref), kband, vband, sem)
    count = build_pairs(pattern_ref, tile_of, place_of, (0, 2))
    top[...] = top_in[...]
    total[...] = total_in[...]
    acc[...] = acc_in[...]
    for copy in copies:
        copy.wait()
    forward_pairs(
        count, q_ref, kband, vband, tile_of, place_of, (s0, m0), (s1, m1), top, total, acc
    )
    for tile in range(ROW_TILES):
        attended = acc[tile] / total[tile]
        flip_ref[tile] = attended.astype(BF)
        att_ref[tile] = attended.T.astype(BF)
        lse_ref[tile] = top[tile] + jnp.log2(total[tile])


def backward_pairs(
    count, q_ref, back, att_ref, lse_ref, kband, vband, tile_of, place_of,
    even, odd, delta, dk, dv, dq,
):
    for tile in range(ROW_TILES):
        prod = back[tile].astype(F32) * att_ref[tile].astype(F32)
        delta[tile] = jnp.sum(prod, axis=0, keepdims=True)

    def make(slot, i):
        tile, place = tile_of[i], place_of[i]
        scores = dot(kband[place], q_ref[tile], NT) * (SCALING * LOG2E)
        prob = jnp.exp2(scores - lse_ref[tile])
        prob_grad = dot(vband[place], back[tile], NN)
        slot[0][...] = prob.astype(BF)
        slot[1][...] = (prob * (prob_grad - delta[tile])).astype(BF)

    def use(slot, i):
        tile, place = tile_of[i], place_of[i]
        dv[place] += dot(slot[0][...], back[tile], NT)
        dk[place] += dot(slot[1][...], q_ref[tile], NN)
        dq[tile] += dot(kband[place], slot[1][...], TN)

    run_pairs(count, make, use, even, odd)


def backward_halo_kernel(
    pattern_ref, q_ref, back_mine_ref, back_got_ref, att_ref, lse_ref, above_ref, below_ref,
    early_ref,
    up_ref, down_ref, dq, back_ref, zero_ref,
    kband, vband, tile_of, place_of, p0, p1, d0, d1, delta, dk, dv, sem,
):
    copies = fill_band((above_ref, below_ref), kband, vband, sem)
    count = build_pairs(pattern_ref, tile_of, place_of, (0, 2))
    dk[...] = jnp.zeros(dk.shape, F32)
    dv[...] = jnp.zeros(dv.shape, F32)
    dq[...] = jnp.zeros(dq.shape, F32)
    zero_ref[...] = jnp.zeros(zero_ref.shape, F32)
    for tile in range(ROW_TILES):
        cols = pl.ds(tile * TILE, TILE)
        back_ref[tile] = (back_mine_ref[:, cols] + back_got_ref[:, cols].astype(F32)).astype(BF)
    for copy in copies:
        copy.wait()
    backward_pairs(
        count, q_ref, back_ref, att_ref, lse_ref, kband, vband, tile_of, place_of,
        (p0, d0), (p1, d1), delta, dk, dv, dq,
    )
    for i in range(ROW_TILES):
        up_ref[0, i] = dk[i].astype(BF)
        up_ref[1, i] = dv[i].astype(BF)
        down_ref[0, i] = dk[ROW_TILES + i].astype(BF)
        down_ref[1, i] = dv[ROW_TILES + i].astype(BF)


def backward_own_kernel(
    pattern_ref, q_ref, back_ref, att_ref, lse_ref, k_ref, v_ref, dq_in, early_ref,
    dq_ref, dk, dv, zero_ref,
    tile_of, place_of, p0, p1, d0, d1, delta, dq,
):
    count = build_pairs(pattern_ref, tile_of, place_of, (1,))
    dk[...] = jnp.zeros(dk.shape, F32)
    dv[...] = jnp.zeros(dv.shape, F32)
    zero_ref[...] = jnp.zeros(zero_ref.shape, F32)
    dq[...] = dq_in[...]
    backward_pairs(
        count, q_ref, back_ref, att_ref, lse_ref, k_ref, v_ref, tile_of, place_of,
        (p0, d0), (p1, d1), delta, dk, dv, dq,
    )
    for tile in range(ROW_TILES):
        dq_ref[tile] = (dq[tile] * SCALING).T.astype(BF)


def made_kernel(*refs):
    zero_ref = refs[-1]
    zero_ref[...] = jnp.zeros(zero_ref.shape, F32)


def weight_kernel(place_ref, grad_ref, att_ref, other_ref, early_ref, send_ref, keep_ref, heads, total):
    half, core = place_ref[0], place_ref[1]
    heads[:, pl.ds(pl.multiple_of(half * HDIM, HDIM), HDIM)] = att_ref[...]
    heads[:, pl.ds(pl.multiple_of((1 - half) * HDIM, HDIM), HDIM)] = other_ref[...]
    total[...] = dot(grad_ref[...], heads[...], NN)
    rows = send_ref.shape[3]
    for low in range(2):
        for xh in range(2):
            chunk = low * 4 + xh * 2
            mine = pl.ds(pl.multiple_of((chunk + core) * rows, 8), rows)
            yours = pl.ds(pl.multiple_of((chunk + 1 - core) * rows, 8), rows)
            for a in range(2):
                lanes = slice(a * HDIM, (a + 1) * HDIM)
                keep_ref[a, low, xh] = total[mine, lanes]
                send_ref[a, low, xh] = total[yours, lanes].astype(BF)


VM = pl.BlockSpec(memory_space=pltpu.VMEM)
SM = pl.BlockSpec(memory_space=pltpu.SMEM)
HB = pl.BlockSpec(memory_space=pltpu.HBM)
BLOCK = (ROW_TILES, TILE, HDIM)
FLIP = (ROW_TILES, HDIM, TILE)
LINE = (ROW_TILES, 1, TILE)
HALO = (2 * ROW_TILES, TILE, HDIM)
PAIR_LISTS = [pltpu.SMEM((49,), jnp.int32), pltpu.SMEM((49,), jnp.int32)]
HALO_BAND = [pltpu.VMEM(HALO, BF), pltpu.VMEM(HALO, BF)]
SCORES = [pltpu.VMEM((TILE, TILE), F32)] * 2 + [pltpu.VMEM((1, TILE), F32)] * 2
TERMS = [pltpu.VMEM((TILE, TILE), BF)] * 4
DMA_SEMS = pltpu.SemaphoreType.DMA((4,))


def kernel_call(kernel, name, outs, in_specs, scratch, flops):
    return pl.pallas_call(
        kernel,
        name=name,
        out_shape=tuple(jax.ShapeDtypeStruct(shape, kind) for shape, kind in outs),
        in_specs=in_specs,
        out_specs=(VM,) * len(outs),
        scratch_shapes=scratch,
        compiler_params=pltpu.CompilerParams(vmem_limit_bytes=32 * 1024 * 1024),
        cost_estimate=pl.CostEstimate(
            flops=flops, bytes_accessed=4_000_000, transcendentals=3_000_000
        ),
    )


def forward_own(*args):
    return kernel_call(
        forward_own_kernel, "forward_own", [(LINE, F32), (LINE, F32), (FLIP, F32)],
        [SM, VM, VM, VM], PAIR_LISTS + SCORES, 3_000_000_000,
    )(*args)


def forward_halo(*args):
    state = [pltpu.VMEM(LINE, F32), pltpu.VMEM(LINE, F32), pltpu.VMEM(FLIP, F32)]
    return kernel_call(
        forward_halo_kernel, "forward_halo", [(BLOCK, BF), (FLIP, BF), (LINE, F32)],
        [SM] + [VM] * 4 + [HB] * 3, HALO_BAND + PAIR_LISTS + SCORES + state + [DMA_SEMS],
        5_000_000_000,
    )(*args)


def backward_halo(*args):
    outs = [((2,) + BLOCK, BF), ((2,) + BLOCK, BF), (FLIP, F32), (FLIP, BF), ((1, HDIM), F32)]
    return kernel_call(
        backward_halo_kernel, "backward_halo", outs, [SM] + [VM] * 5 + [HB] * 3,
        HALO_BAND + PAIR_LISTS + TERMS
        + [pltpu.VMEM(LINE, F32), pltpu.VMEM(HALO, F32), pltpu.VMEM(HALO, F32), DMA_SEMS],
        12_000_000_000,
    )(*args)


def backward_own(*args):
    outs = [(BLOCK, BF), (BLOCK, F32), (BLOCK, F32), ((1, HDIM), F32)]
    return kernel_call(
        backward_own_kernel, "backward_own", outs, [SM] + [VM] * 7 + [HB],
        PAIR_LISTS + TERMS + [pltpu.VMEM(LINE, F32), pltpu.VMEM(FLIP, F32)],
        6_000_000_000,
    )(*args)


def made(*arrays):
    any_space = pl.BlockSpec(memory_space=pl.ANY)
    return kernel_call(made_kernel, "made", [((1, HDIM), F32)], [any_space] * len(arrays), [], 1000)(*arrays)[0]


def weight_parts(place, grad_half, att, att_other, early):
    feats, tokens = grad_half.shape
    shape = (2, 2, 2, feats // 8, HDIM)
    return kernel_call(
        weight_kernel, "weight_parts", [(shape, BF), (shape, F32)], [SM] + [VM] * 3 + [HB],
        [pltpu.VMEM((tokens, 2 * HDIM), BF), pltpu.VMEM((feats, 2 * HDIM), F32)],
        2_000_000_000,
    )(place, grad_half, att, att_other, early)


def shifted(block, distance):
    route = [(i - distance, i) for i in range(16) if 0 <= i - distance < 16]
    return lax.ppermute(block, ST, route)


def swapped(block):
    return lax.ppermute(block, "xl", [(0, 1), (1, 0)])


def halved(part, axis, distance, size, dim, bit):
    route = [(i, i ^ distance) for i in range(size)]
    send = lax.dynamic_index_in_dim(part, 1 - bit, dim, keepdims=False).astype(BF)
    keep = lax.dynamic_index_in_dim(part, bit, dim, keepdims=False)
    return keep, lax.ppermute(send, axis, route)


def body(queries, key_rows, value_rows, out_grad, proj_weight, pattern):
    half, y = lax.axis_index("xl"), lax.axis_index("y")
    tokens = queries.shape[1]
    place = jnp.stack((half, lax.axis_index("core"))).astype(jnp.int32)
    q = queries.reshape(BLOCK)
    keys, values = key_rows.reshape(BLOCK), value_rows.reshape(BLOCK)
    kv = jnp.stack((keys, values))
    above, below = shifted(kv, 1), shifted(kv, -1)

    grad_half = lax.all_gather(out_grad[0].T, "z", axis=0, tiled=True)
    feats = grad_half.shape[0]
    w_mine = lax.dynamic_slice_in_dim(proj_weight, half * feats, feats, 1)
    w_other = swapped(lax.dynamic_slice_in_dim(proj_weight, (1 - half) * feats, feats, 1))

    own_state = forward_own(pattern, q, keys, values)
    attended, att_flip, lse = forward_halo(pattern, q, *own_state, above, below, w_other)
    att = attended.reshape(tokens, HDIM)
    att_other = swapped(att)

    back_sent = dot(w_other, grad_half, NN).astype(BF)
    back_got = swapped(back_sent)
    back_mine = dot(w_mine, grad_half, NN)

    sent, kept = weight_parts(place, grad_half, att, att_other, back_sent)
    got = lax.ppermute(sent, "core", [(0, 1), (1, 0)])
    kept, got = halved(kept + got.astype(F32), "xh", 1, 2, 2, lax.axis_index("xh"))

    by_rows = (((0,), (1,)), ((), ()))
    part = dot(w_mine, att, by_rows) + dot(w_other, att_other, by_rows)
    part = part + made(back_got, kept)[:, :1]
    projected = lax.psum_scatter(part.astype(BF), "z", scatter_dimension=0, tiled=True)
    projected = projected.T[None]

    up, down, dq_part, back, _ = backward_halo(
        pattern, q, back_mine, back_got, att_flip, lse, above, below, sent
    )
    up, down = shifted(up, -1), shifted(down, 1)
    dq, dk, dv, zero = backward_own(pattern, q, back, att_flip, lse, keys, values, dq_part, kept)

    kept = (kept + got.astype(F32) + zero).astype(BF).reshape((4,) + kept.shape[2:])
    summed = 0.0
    for k in range(4):
        piece = lax.dynamic_index_in_dim(kept, y ^ k, 0, keepdims=False)
        route = [
            (h * 4 + i, (i ^ k) // 2 * 4 + 2 * h + (i ^ k) % 2) for h in range(2) for i in range(4)
        ]
        summed = summed + lax.ppermute(piece, ("xl", "y"), route).astype(F32)
    weight_grad = summed.T

    shape = (1, tokens, HDIM)
    key_grad = SCALING * (dk + up[0].astype(F32) + down[0].astype(F32))
    value_grad = dv + up[1].astype(F32) + down[1].astype(F32)
    key_grad = key_grad.astype(BF).reshape(shape)
    value_grad = value_grad.astype(BF).reshape(shape)
    return projected, dq.reshape(shape), key_grad, value_grad, weight_grad


def solution(mesh):
    fine = Mesh(mesh.devices.reshape(2, 8, 4, 2, 2), ("xl", "z", "y", "xh", "core"))
    fsdp = ("xl", "z")
    rows = P(None, ST, fsdp)
    return jax.shard_map(
        body,
        mesh=fine,
        in_specs=(rows, rows, rows, rows, P(fsdp, None), P(ST, None)),
        out_specs=(rows, rows, rows, rows, P(fsdp, ST)),
        check_vma=False,
    )
```

```python
import functools

import jax
import jax.numpy as jnp
from jax import lax
from jax.experimental import pallas as pl
from jax.experimental.pallas import tpu as pltpu
from jax.sharding import Mesh
from jax.sharding import PartitionSpec as P

HDIM = 128
TILE = 384
TF = 2
TC = 2
ROW_TILES = TF * TC
BAND = 3 * ROW_TILES
SCALING = HDIM ** (-0.5)
LOG2E = 1.4426950408889634
BF = jnp.bfloat16
F32 = jnp.float32
ST = ("y", "xh", "core")
NT = (((1,), (1,)), ((), ()))
TN = (((0,), (0,)), ((), ()))
NN = (((1,), (0,)), ((), ()))


def dot(a, b, dims):
    return lax.dot_general(a, b, dims, preferred_element_type=F32)


def build_pairs(pattern_ref, tile_of, place_of, rows):
    count = jnp.int32(0)
    for tile in range(ROW_TILES):
        frame, col = tile // TC, tile % TC
        for at, row in enumerate(rows):
            for inner in range(ROW_TILES):
                slot = (inner // TC - frame + 1) * 9 + row * 3 + (inner % TC - col + 1)
                tile_of[count] = jnp.int32(tile)
                place_of[count] = jnp.int32(at * ROW_TILES + inner)
                count = count + (pattern_ref[tile, slot] >= 0).astype(jnp.int32)
    return count


def run_pairs(count, make, use, even, odd):
    make(even, 0)

    def step(j, carry):
        i = 2 * j
        make(odd, i + 1)
        use(even, i)
        make(even, i + 2)
        use(odd, i + 1)
        return carry

    lax.fori_loop(0, (count - 1) // 2, step, 0)

    @pl.when(count % 2 == 1)
    def _():
        use(even, count - 1)

    @pl.when(count % 2 == 0)
    def _():
        make(odd, count - 1)
        use(even, count - 2)
        use(odd, count - 1)


def fill_band(refs, kband, vband, sem):
    copies = []
    for i, ref in enumerate(refs):
        place = pl.ds(i * ROW_TILES, ROW_TILES)
        copies.append(pltpu.make_async_copy(ref[0], kband.at[place], sem.at[2 * i]))
        copies.append(pltpu.make_async_copy(ref[1], vband.at[place], sem.at[2 * i + 1]))
    for copy in copies:
        copy.start()
    return copies


def forward_pairs(count, q_ref, kband, vband, tile_of, place_of, even, odd, top, total, acc):
    def make(slot, i):
        scores = dot(kband[place_of[i]], q_ref[tile_of[i]], NT) * (SCALING * LOG2E)
        slot[0][...] = scores
        slot[1][...] = jnp.max(scores, axis=0, keepdims=True)

    def use(slot, i):
        tile = tile_of[i]
        before = top[tile]
        peak = jnp.maximum(before, slot[1][...])
        shrink = jnp.exp2(before - peak)
        raised = jnp.exp2(slot[0][...] - peak)
        top[tile] = peak
        total[tile] = shrink * total[tile] + jnp.sum(raised, axis=0, keepdims=True)
        acc[tile] = shrink * acc[tile] + dot(vband[place_of[i]], raised.astype(BF), TN)

    run_pairs(count, make, use, even, odd)


def forward_own_kernel(
    pattern_ref, q_ref, k_ref, v_ref, top, total, acc, tile_of, place_of, s0, s1, m0, m1
):
    count = build_pairs(pattern_ref, tile_of, place_of, (1,))
    top[...] = jnp.full(top.shape, -jnp.inf, F32)
    total[...] = jnp.zeros(total.shape, F32)
    acc[...] = jnp.zeros(acc.shape, F32)
    forward_pairs(
        count, q_ref, k_ref, v_ref, tile_of, place_of, (s0, m0), (s1, m1), top, total, acc
    )


def forward_halo_kernel(
    pattern_ref, q_ref, top_in, total_in, acc_in, ka_ref, va_ref, kb_ref, vb_ref, early_ref,
    att_ref, flip_ref, lse_ref,
    kband, vband, tile_of, place_of, s0, s1, m0, m1, top, total, acc, sem,
):
    copies = fill_band(((ka_ref, va_ref), (kb_ref, vb_ref)), kband, vband, sem)
    count = build_pairs(pattern_ref, tile_of, place_of, (0, 2))
    top[...] = top_in[...]
    total[...] = total_in[...]
    acc[...] = acc_in[...]
    for copy in copies:
        copy.wait()
    forward_pairs(
        count, q_ref, kband, vband, tile_of, place_of, (s0, m0), (s1, m1), top, total, acc
    )
    for tile in range(ROW_TILES):
        attended = acc[tile] / total[tile]
        flip_ref[tile] = attended.astype(BF)
        att_ref[tile] = attended.T.astype(BF)
        lse_ref[tile] = top[tile] + jnp.log2(total[tile])


def backward_pairs(
    count, q_ref, back, att_ref, lse_ref, kband, vband, tile_of, place_of,
    even, odd, delta, dk, dv, dq,
):
    for tile in range(ROW_TILES):
        prod = back[tile].astype(F32) * att_ref[tile].astype(F32)
        delta[tile] = jnp.sum(prod, axis=0, keepdims=True)

    def make(slot, i):
        tile, place = tile_of[i], place_of[i]
        scores = dot(kband[place], q_ref[tile], NT) * (SCALING * LOG2E)
        prob = jnp.exp2(scores - lse_ref[tile])
        prob_grad = dot(vband[place], back[tile], NN)
        slot[0][...] = prob.astype(BF)
        slot[1][...] = (prob * (prob_grad - delta[tile])).astype(BF)

    def use(slot, i):
        tile, place = tile_of[i], place_of[i]
        dv[place] += dot(slot[0][...], back[tile], NT)
        dk[place] += dot(slot[1][...], q_ref[tile], NN)
        dq[tile] += dot(kband[place], slot[1][...], TN)

    run_pairs(count, make, use, even, odd)


def backward_halo_kernel(
    pattern_ref, q_ref, back_mine_ref, back_got_ref, att_ref, lse_ref, ka_ref, va_ref, kb_ref, vb_ref,
    early_ref,
    up_ref, down_ref, dq, back_ref, zero_ref,
    kband, vband, tile_of, place_of, p0, p1, d0, d1, delta, dk, dv, sem,
):
    copies = fill_band(((ka_ref, va_ref), (kb_ref, vb_ref)), kband, vband, sem)
    count = build_pairs(pattern_ref, tile_of, place_of, (0, 2))
    dk[...] = jnp.zeros(dk.shape, F32)
    dv[...] = jnp.zeros(dv.shape, F32)
    dq[...] = jnp.zeros(dq.shape, F32)
    zero_ref[...] = jnp.zeros(zero_ref.shape, F32)
    for tile in range(ROW_TILES):
        cols = pl.ds(tile * TILE, TILE)
        back_ref[tile] = (back_mine_ref[:, cols] + back_got_ref[:, cols].astype(F32)).astype(BF)
    for copy in copies:
        copy.wait()
    backward_pairs(
        count, q_ref, back_ref, att_ref, lse_ref, kband, vband, tile_of, place_of,
        (p0, d0), (p1, d1), delta, dk, dv, dq,
    )
    for i in range(ROW_TILES):
        up_ref[0, i] = dk[i].astype(BF)
        up_ref[1, i] = dv[i].astype(BF)
        down_ref[0, i] = dk[ROW_TILES + i].astype(BF)
        down_ref[1, i] = dv[ROW_TILES + i].astype(BF)


def backward_own_kernel(
    pattern_ref, q_ref, back_ref, att_ref, lse_ref, k_ref, v_ref, dq_in, early_ref,
    dq_ref, dk, dv, zero_ref,
    tile_of, place_of, p0, p1, d0, d1, delta, dq,
):
    count = build_pairs(pattern_ref, tile_of, place_of, (1,))
    dk[...] = jnp.zeros(dk.shape, F32)
    dv[...] = jnp.zeros(dv.shape, F32)
    zero_ref[...] = jnp.zeros(zero_ref.shape, F32)
    dq[...] = dq_in[...]
    backward_pairs(
        count, q_ref, back_ref, att_ref, lse_ref, k_ref, v_ref, tile_of, place_of,
        (p0, d0), (p1, d1), delta, dk, dv, dq,
    )
    for tile in range(ROW_TILES):
        dq_ref[tile] = (dq[tile] * SCALING).T.astype(BF)


def made_kernel(array_ref, zero_ref):
    zero_ref[...] = jnp.zeros(zero_ref.shape, F32)


def weight_kernel(place_ref, grad_ref, att_ref, other_ref, early_ref, send_ref, keep_ref, heads, total):
    half, core = place_ref[0], place_ref[1]
    heads[:, pl.ds(pl.multiple_of(half * HDIM, HDIM), HDIM)] = att_ref[...]
    heads[:, pl.ds(pl.multiple_of((1 - half) * HDIM, HDIM), HDIM)] = other_ref[...]
    total[...] = dot(grad_ref[...], heads[...], NN)
    rows = send_ref.shape[3]
    for low in range(2):
        for xh in range(2):
            chunk = low * 4 + xh * 2
            mine = pl.ds(pl.multiple_of((chunk + core) * rows, 8), rows)
            yours = pl.ds(pl.multiple_of((chunk + 1 - core) * rows, 8), rows)
            for a in range(2):
                lanes = slice(a * HDIM, (a + 1) * HDIM)
                keep_ref[a, low, xh] = total[mine, lanes]
                send_ref[a, low, xh] = total[yours, lanes].astype(BF)


VM = pl.BlockSpec(memory_space=pltpu.VMEM)
SM = pl.BlockSpec(memory_space=pltpu.SMEM)
HB = pl.BlockSpec(memory_space=pltpu.HBM)
BLOCK = (ROW_TILES, TILE, HDIM)
FLIP = (ROW_TILES, HDIM, TILE)
LINE = (ROW_TILES, 1, TILE)
HALO = (2 * ROW_TILES, TILE, HDIM)
PAIR_LISTS = [pltpu.SMEM((49,), jnp.int32), pltpu.SMEM((49,), jnp.int32)]
HALO_BAND = [pltpu.VMEM(HALO, BF), pltpu.VMEM(HALO, BF)]
SCORES = [pltpu.VMEM((TILE, TILE), F32)] * 2 + [pltpu.VMEM((1, TILE), F32)] * 2
TERMS = [pltpu.VMEM((TILE, TILE), BF)] * 4
DMA_SEMS = pltpu.SemaphoreType.DMA((4,))


def kernel_call(kernel, name, outs, in_specs, scratch, flops):
    return pl.pallas_call(
        kernel,
        name=name,
        out_shape=tuple(jax.ShapeDtypeStruct(shape, kind) for shape, kind in outs),
        in_specs=in_specs,
        out_specs=(VM,) * len(outs),
        scratch_shapes=scratch,
        compiler_params=pltpu.CompilerParams(vmem_limit_bytes=32 * 1024 * 1024),
        cost_estimate=pl.CostEstimate(
            flops=flops, bytes_accessed=4_000_000, transcendentals=3_000_000
        ),
    )


def forward_own(*args):
    return kernel_call(
        forward_own_kernel, "forward_own", [(LINE, F32), (LINE, F32), (FLIP, F32)],
        [SM, VM, VM, VM], PAIR_LISTS + SCORES, 3_000_000_000,
    )(*args)


def forward_halo(*args):
    state = [pltpu.VMEM(LINE, F32), pltpu.VMEM(LINE, F32), pltpu.VMEM(FLIP, F32)]
    return kernel_call(
        forward_halo_kernel, "forward_halo", [(BLOCK, BF), (FLIP, BF), (LINE, F32)],
        [SM] + [VM] * 4 + [HB] * 5, HALO_BAND + PAIR_LISTS + SCORES + state + [DMA_SEMS],
        5_000_000_000,
    )(*args)


def backward_halo(*args):
    outs = [((2,) + BLOCK, BF), ((2,) + BLOCK, BF), (FLIP, F32), (FLIP, BF), ((1, HDIM), F32)]
    return kernel_call(
        backward_halo_kernel, "backward_halo", outs, [SM] + [VM] * 5 + [HB] * 5,
        HALO_BAND + PAIR_LISTS + TERMS
        + [pltpu.VMEM(LINE, F32), pltpu.VMEM(HALO, F32), pltpu.VMEM(HALO, F32), DMA_SEMS],
        12_000_000_000,
    )(*args)


def backward_own(*args):
    outs = [(BLOCK, BF), (BLOCK, F32), (BLOCK, F32), ((1, HDIM), F32)]
    return kernel_call(
        backward_own_kernel, "backward_own", outs, [SM] + [VM] * 7 + [HB],
        PAIR_LISTS + TERMS + [pltpu.VMEM(LINE, F32), pltpu.VMEM(FLIP, F32)],
        6_000_000_000,
    )(*args)


def made(array):
    any_space = pl.BlockSpec(memory_space=pl.ANY)
    return kernel_call(made_kernel, "made", [((1, HDIM), F32)], [any_space], [], 1000)(array)[0]


def weight_parts(place, grad_half, att, att_other, early):
    feats, tokens = grad_half.shape
    shape = (2, 2, 2, feats // 8, HDIM)
    return kernel_call(
        weight_kernel, "weight_parts", [(shape, BF), (shape, F32)], [SM] + [VM] * 3 + [HB],
        [pltpu.VMEM((tokens, 2 * HDIM), BF), pltpu.VMEM((feats, 2 * HDIM), F32)],
        2_000_000_000,
    )(place, grad_half, att, att_other, early)


def shifted(block, distance):
    route = [(i - distance, i) for i in range(16) if 0 <= i - distance < 16]
    return lax.ppermute(block, ST, route)


def swapped(block):
    return lax.ppermute(block, "xl", [(0, 1), (1, 0)])


def halved(part, axis, distance, size, dim, bit):
    route = [(i, i ^ distance) for i in range(size)]
    send = lax.dynamic_index_in_dim(part, 1 - bit, dim, keepdims=False).astype(BF)
    keep = lax.dynamic_index_in_dim(part, bit, dim, keepdims=False)
    return keep, lax.ppermute(send, axis, route)


def body(queries, key_rows, value_rows, out_grad, proj_weight, pattern):
    half, y = lax.axis_index("xl"), lax.axis_index("y")
    tokens = queries.shape[1]
    place = jnp.stack((half, lax.axis_index("core"))).astype(jnp.int32)
    q = queries.reshape(BLOCK)
    keys, values = key_rows.reshape(BLOCK), value_rows.reshape(BLOCK)
    above = shifted(keys, 1), shifted(values, 1)
    below = shifted(keys, -1), shifted(values, -1)

    grad_half = lax.all_gather(out_grad[0].T, "z", axis=0, tiled=True)
    feats = grad_half.shape[0]
    w_mine = lax.dynamic_slice_in_dim(proj_weight, half * feats, feats, 1)
    w_other = swapped(lax.dynamic_slice_in_dim(proj_weight, (1 - half) * feats, feats, 1))

    own_state = forward_own(pattern, q, keys, values)
    attended, att_flip, lse = forward_halo(pattern, q, *own_state, *above, *below, w_other)
    att = attended.reshape(tokens, HDIM)
    att_other = swapped(att)

    back_sent = dot(w_other, grad_half, NN).astype(BF)
    back_got = swapped(back_sent)
    back_mine = dot(w_mine, grad_half, NN)

    by_rows = (((0,), (1,)), ((), ()))
    part = dot(w_mine, att, by_rows) + dot(w_other, att_other, by_rows)
    part = part + made(back_sent)[:, :1]
    projected = lax.psum_scatter(part.astype(BF), "z", scatter_dimension=0, tiled=True)
    projected = projected.T[None]

    sent, kept = weight_parts(place, grad_half, att, att_other, back_sent)
    got = lax.ppermute(sent, "core", [(0, 1), (1, 0)])
    kept, got = halved(kept + got.astype(F32), "xh", 1, 2, 2, lax.axis_index("xh"))

    up, down, dq_part, back, _ = backward_halo(
        pattern, q, back_mine, back_got, att_flip, lse, *above, *below, sent
    )
    up, down = shifted(up, -1), shifted(down, 1)
    dq, dk, dv, zero = backward_own(pattern, q, back, att_flip, lse, keys, values, dq_part, kept)

    kept = (kept + got.astype(F32) + zero).astype(BF).reshape((4,) + kept.shape[2:])
    summed = 0.0
    for k in range(4):
        piece = lax.dynamic_index_in_dim(kept, y ^ k, 0, keepdims=False)
        route = [
            (h * 4 + i, (i ^ k) // 2 * 4 + 2 * h + (i ^ k) % 2) for h in range(2) for i in range(4)
        ]
        summed = summed + lax.ppermute(piece, ("xl", "y"), route).astype(F32)
    weight_grad = summed.T

    shape = (1, tokens, HDIM)
    key_grad = SCALING * (dk + up[0].astype(F32) + down[0].astype(F32))
    value_grad = dv + up[1].astype(F32) + down[1].astype(F32)
    key_grad = key_grad.astype(BF).reshape(shape)
    value_grad = value_grad.astype(BF).reshape(shape)
    return projected, dq.reshape(shape), key_grad, value_grad, weight_grad


def solution(mesh):
    fine = Mesh(mesh.devices.reshape(2, 8, 4, 2, 2), ("xl", "z", "y", "xh", "core"))
    fsdp = ("xl", "z")
    rows = P(None, ST, fsdp)
    return jax.shard_map(
        body,
        mesh=fine,
        in_specs=(rows, rows, rows, rows, P(fsdp, None), P(ST, None)),
        out_specs=(rows, rows, rows, rows, P(fsdp, ST)),
        check_vma=False,
    )
```
